32 devices in a mesh: groups: 2 (over y), replica: 4 (over z), tensor: 4 (over x, core).
Axes of the slice: x: 2, y: 2, z: 4, core: 2. Of those that a mesh axis runs over, the one named last changes fastest.
Arguments:
- hidden_input_saved: bfloat16 [4096, 5120], P(('groups', 'replica'), 'tensor'), parts along dimension 0, may hold values from -6 to 6
- value_output_gradient: bfloat16 [4096, 512], P(('groups', 'replica'), 'tensor'), parts along dimension 0, may hold values from -6 to 6
- frozen_value_weight: bfloat16 [5120, 512], P('tensor'), may hold values from -0.078125 to 0.078125
- adapter_lower_factor: bfloat16 [32, 16, 5120], P(('groups', 'replica'), None, 'tensor'), parts along dimension 0, may hold values from -0.078125 to 0.078125
- adapter_upper_factor: bfloat16 [32, 16, 512], P(('groups', 'replica'), None, 'tensor'), parts along dimension 0, may hold values from -1.5 to 1.5
- per_token_adapter: int32 [4096, 1], P(('groups', 'replica')), parts along dimension 0, may hold values from 0 to 15; in each aligned block of 512 rows (0 to 511, 512 to 1023, ...) at most 96 rows name the same one
- adapter_table_slot: int32 [32], P('groups'), parts along dimension 0, may hold values from 0 to 15, each once
Outputs:
- hidden_grad: bfloat16 [4096, 5120], P(('groups', 'replica'), 'tensor'), parts along dimension 0
- down_grad: bfloat16 [32, 16, 5120], P(('groups', 'replica'), None, 'tensor'), parts along dimension 0
- up_grad: bfloat16 [32, 16, 512], P(('groups', 'replica'), None, 'tensor'), parts along dimension 0
The draws below stay inside these ranges and needn't reach their ends.
There are 2 independent parts, one for each index of `groups`. The reference program is written for one: setup_inputs(seed, part) draws one part's arguments, and reference() takes and returns one part's arrays. A program takes and returns all parts, laid end to end along the dimension named above; an argument that names none is the same for every part. Nothing has to cross between parts.
Inputs may be any that keep to these rules, and one draw needn't show every extreme that they name: `per_token_adapter`: every adapter is named by some token. Among the tokens of one index of replica at most 96 name the same adapter, a bound that some block reaches there. `adapter_table_slot`: each adapter has one slot; slot i is held by replica index i // 4.
All inputs are finite; a program needn't handle non-finite values.
Results may differ from the reference program's by a relative error of at most 0.0055.
Values may be sent and summed in bfloat16 or wider, within the bound.
A program may use at most 64 MiB of HBM per device.

```python
import math
import jax
import jax.numpy as jnp
import numpy as np
from jax import lax

MODEL_WIDTH = 5120
VALUE_FEATURES = 512
ADAPTER_RANK = 16
TOK_DEV = 512
ADAPTER_TOTAL = 16
CAPA = 96
TOKENS = 2048


def level_of(rng, dims, pieces, low, high):
    factor_of = 1.0
    for dim, blocks in pieces:
        draws = jax.random.uniform(jax.random.fold_in(jax.random.fold_in(rng, 6), dim), (blocks,), jnp.float32, low / len(pieces), high / len(pieces))
        factor_of = factor_of * jnp.repeat(jnp.exp(draws), dims[dim] // blocks).reshape((-1,) + (1,) * (len(dims) - 1 - dim))
    return factor_of


def assign_block(rng, own, number, rows, number_of, top, bound, lean):
    sequence = jax.random.permutation(rng, number_of)
    crowded, common = portions_of(number_of, rows * top, bound, lean, True), portions_of(number_of, rows * top, bound, lean, False)
    places = jnp.arange(number_of)

    def named(sizes, offset_by):
        used = int((sizes > 0).sum())
        fixed = max(1, used // 4)
        moved = fixed + (places - fixed + offset_by * (used - fixed)) % max(1, number_of - fixed)
        return jnp.zeros((number_of,), jnp.int32).at[sequence[jnp.where(places < fixed, places, moved)]].set(jnp.asarray(sizes, jnp.int32))

    sizes = jnp.where(number % 4 == 0, named(crowded, number // 4), named(common, number - number // 4 - 1))
    mixed = jax.random.permutation(jax.random.fold_in(own, 3), number_of)
    giver, sink = mixed[0:number_of // 2 * 2:2], mixed[1:number_of // 2 * 2:2]
    room = jnp.minimum(sizes[giver] - 1, bound - sizes[sink]) // 2
    room = jnp.where((giver == sequence[0]) | (sink == sequence[0]) | (sizes[sink] == 0), 0, jnp.maximum(room, 0))
    moved = jax.random.randint(jax.random.fold_in(own, 4), (number_of // 2,), 0, 1 << 20) % (room + 1)
    sizes = sizes.at[giver].add(-moved).at[sink].add(moved)
    members = jnp.searchsorted(jnp.cumsum(sizes), jnp.arange(rows * top), side="right").astype(jnp.int32)
    table = members.reshape(top, rows).T
    table = table[jax.random.permutation(jax.random.fold_in(own, 1), rows)]
    offset_by = jax.random.randint(jax.random.fold_in(own, 2), (rows, 1), 0, top)
    return jnp.take_along_axis(table, (jnp.arange(top)[None, :] + offset_by) % top, axis=1)


def portions_of(amount, total, reach, lean, full):
    loads = [(1 << 20) // math.isqrt(grade ** lean) + 1 for grade in range(1, amount + 1)]
    largest = reach if full else min(reach, max(-(-total // amount), total * loads[0] // sum(loads)))
    least = 1 if total - largest >= amount - 1 else 0
    holding, rest = [largest] + [least] * (amount - 1), total - largest - least * (amount - 1)
    while rest > 0:
        candidates = [i for i in range(1, amount) if holding[i] < largest] or [i for i in range(1, amount) if holding[i] < reach]
        whole, remaining = sum([loads[i] for i in candidates]), rest
        for i in candidates:
            addition = min(reach - holding[i], max(1, remaining * loads[i] // whole), rest)
            holding[i] = holding[i] + addition
            rest = rest - addition
    return np.array(holding)


def noise(key, dims, scale, bound, cuts=(), dtype=jnp.bfloat16):
    values = scale * jax.random.normal(key, dims, jnp.float32)
    if cuts:
        values = values * level_of(key, dims, cuts, -0.22, 0.18)
    return jnp.clip(values, -bound, bound).astype(dtype)


def setup_inputs(seed: int = 0, part: int = 0) -> dict:
    arg_keys = jax.random.split(jax.random.key(seed), 8)
    own_keys = jax.random.split(jax.random.fold_in(arg_keys[7], part), 8)
    hidden_input_saved = noise(own_keys[0], (TOKENS, MODEL_WIDTH), 1.0, 6.0, ((0, 4), (1, 4)))
    value_output_gradient = noise(own_keys[1], (TOKENS, VALUE_FEATURES), 1.0, 6.0, ((0, 4), (1, 4)))
    frozen_value_weight = noise(arg_keys[2], (MODEL_WIDTH, VALUE_FEATURES), MODEL_WIDTH ** -0.5, 0.078125, ((0, 4),))
    adapter_lower_factor = noise(own_keys[3], (ADAPTER_TOTAL, ADAPTER_RANK, MODEL_WIDTH), MODEL_WIDTH ** -0.5, 0.078125, ((0, 4), (2, 4)))
    adapter_upper_factor = noise(own_keys[4], (ADAPTER_TOTAL, ADAPTER_RANK, VALUE_FEATURES), ADAPTER_RANK ** -0.5, 1.5, ((0, 4), (2, 4)))
    per_token_adapter_keys = jax.random.split(jax.random.fold_in(own_keys[5], 1), TOKENS // TOK_DEV)
    per_token_adapter_turns = jax.random.permutation(jax.random.fold_in(own_keys[5], 3), TOKENS // TOK_DEV)
    per_token_adapter = jax.vmap(lambda own, number: assign_block(jax.random.fold_in(own_keys[5], 2), own, number, TOK_DEV, ADAPTER_TOTAL, 1, CAPA, 1))(per_token_adapter_keys, per_token_adapter_turns).reshape((TOKENS, 1))
    adapter_table_slot = jax.random.permutation(own_keys[6], ADAPTER_TOTAL).astype(jnp.int32)
    return dict(hidden_input_saved=hidden_input_saved, value_output_gradient=value_output_gradient, frozen_value_weight=frozen_value_weight, adapter_lower_factor=adapter_lower_factor, adapter_upper_factor=adapter_upper_factor, per_token_adapter=per_token_adapter, adapter_table_slot=adapter_table_slot)


SCALING = 2.0


def reference(hidden_input_saved, value_output_gradient, frozen_value_weight, adapter_lower_factor, adapter_upper_factor, per_token_adapter, adapter_table_slot):
    slot_ids = adapter_table_slot[per_token_adapter[:, 0]].astype(jnp.int32)
    blocks = TOKENS // TOK_DEV
    rows_all = hidden_input_saved.reshape(blocks, TOK_DEV, MODEL_WIDTH)
    values_all = value_output_gradient.reshape(blocks, TOK_DEV, VALUE_FEATURES)
    slots_all = slot_ids.reshape(blocks, TOK_DEV)

    def step(carry, block):
        grad_down, grad_up, counts = carry
        rows, values, token_slots = block
        lower_factor_chosen = adapter_lower_factor[token_slots].astype(jnp.float32)
        upper_factor_chosen = adapter_upper_factor[token_slots].astype(jnp.float32)
        rows_f = rows.astype(jnp.float32)
        values_f = values.astype(jnp.float32)
        coeff_down = lax.optimization_barrier(jnp.einsum("td,trd->tr", rows_f, lower_factor_chosen).astype(jnp.bfloat16))
        upper_coefficient = lax.optimization_barrier(jnp.einsum("te,tre->tr", values_f, upper_factor_chosen).astype(jnp.bfloat16))
        product = lax.optimization_barrier(jnp.einsum("tr,trd->td", upper_coefficient.astype(jnp.float32), lower_factor_chosen).astype(jnp.bfloat16))
        base_grad = jnp.dot(values, frozen_value_weight.T, preferred_element_type=jnp.float32)
        hidden_grad = (base_grad + SCALING * product.astype(jnp.float32)).astype(jnp.bfloat16)
        outer_down = jnp.einsum("tr,td->trd", upper_coefficient.astype(jnp.float32), rows_f)
        outer_up = jnp.einsum("tr,te->tre", coeff_down.astype(jnp.float32), values_f)
        grad_down = grad_down + jax.ops.segment_sum(outer_down, token_slots, num_segments=ADAPTER_TOTAL)
        grad_up = grad_up + jax.ops.segment_sum(outer_up, token_slots, num_segments=ADAPTER_TOTAL)
        counts = counts + jax.ops.segment_sum(jnp.ones(token_slots.shape, jnp.float32), token_slots, num_segments=ADAPTER_TOTAL)
        return (grad_down, grad_up, counts), hidden_grad

    start = (jnp.zeros((ADAPTER_TOTAL, ADAPTER_RANK, MODEL_WIDTH), jnp.float32), jnp.zeros((ADAPTER_TOTAL, ADAPTER_RANK, VALUE_FEATURES), jnp.float32), jnp.zeros((ADAPTER_TOTAL,), jnp.float32))
    (grad_down, grad_up, counts), hidden_blocks = lax.scan(step, start, (rows_all, values_all, slots_all))
    factor = SCALING / counts
    down_grad = (grad_down * factor[:, None, None]).astype(jnp.bfloat16)
    up_grad = (grad_up * factor[:, None, None]).astype(jnp.bfloat16)
    return hidden_blocks.reshape(TOKENS, MODEL_WIDTH), down_grad, up_grad
```

```python
import functools
import math

import jax
import jax.numpy as jnp
from jax import lax
from jax.experimental import pallas as pl
from jax.experimental.pallas import tpu as pltpu
from jax.sharding import PartitionSpec as P

SCALING = 2.0

MESH = pl.DeviceIdType.MESH
F32 = jnp.float32
BF16 = jnp.bfloat16


def fused_body(
    replicas,
    tensors,
    owned,
    x_hbm,
    v_hbm,
    w_hbm,
    a_hbm,
    b_hbm,
    ids_ref,
    table_ref,
    hid_hbm,
    down_ref,
    up_ref,
    x,
    w,
    v_own,
    v_full,
    a_all,
    b_all,
    hid,
    cu_all,
    cd_all,
    cm,
    cmt,
    part,
    snd,
    hop_r,
    hop_l,
    up_part,
    up_all,
    cnt_part,
    cnt_all,
    load_sem,
    a_send_r,
    a_send_l,
    a_recv,
    rs_send,
    rs_recv_r,
    rs_recv_l,
    b_send,
    b_recv,
    v_send,
    v_recv,
    cu_send,
    cu_recv,
    cd_send,
    cd_recv,
    up_send,
    up_recv,
    cnt_send,
    cnt_recv,
):
    R, T = replicas, tensors
    me = lax.axis_index("replica")
    mt = lax.axis_index("tensor")
    rows = a_hbm.shape[0]
    rank = rows // owned
    tokens, width = x_hbm.shape
    vshare = v_hbm.shape[1]
    adapters = R * owned

    def remote(src, dst, send, recv, axis, to):
        return pltpu.make_async_remote_copy(
            src_ref=src, dst_ref=dst, send_sem=send, recv_sem=recv,
            device_id={axis: to}, device_id_type=MESH,
        )

    def peers(axis):
        n, here = (R, me) if axis == "replica" else (T, mt)
        return [lax.rem(here + d, n) for d in range(1, n)]

    def vcols(i):
        return v_full.at[:, pl.ds(pl.multiple_of(i * vshare, vshare), vshare)]

    loads = {
        "b": pltpu.make_async_copy(b_hbm, b_all.at[me], load_sem.at[0]),
        "v": pltpu.make_async_copy(v_hbm, v_own, load_sem.at[1]),
        "x": pltpu.make_async_copy(x_hbm, x, load_sem.at[2]),
        "a": pltpu.make_async_copy(a_hbm, a_all.at[me], load_sem.at[3]),
        "vf": pltpu.make_async_copy(v_hbm, vcols(mt), load_sem.at[4]),
        "w": pltpu.make_async_copy(w_hbm, w, load_sem.at[5]),
    }
    for name in ("b", "v", "x", "a", "vf", "w"):
        loads[name].start()

    barrier = pltpu.get_barrier_semaphore()
    for axis in ("replica", "tensor"):
        for to in peers(axis):
            pl.semaphore_signal(barrier, inc=1, device_id={axis: to}, device_id_type=MESH)

    ids = ids_ref[...]
    slot = jnp.zeros_like(ids)
    for i in range(adapters):
        slot = jnp.where(ids == i, table_ref[i], slot)
    slot = jnp.broadcast_to(slot, (rank, tokens))
    pad = cnt_part.shape[1]
    for j in range(R):
        which = lax.broadcasted_iota(jnp.int32, (pad, tokens), 0)
        hit = (slot[0:pad, :] == which + j * owned) & (which < owned)
        total = jnp.sum(hit.astype(F32), axis=1, keepdims=True)
        cnt_part[j] = jnp.broadcast_to(total, (pad, 128))

    pl.semaphore_wait(barrier, R - 1 + T - 1)

    b_out = [
        remote(b_hbm, b_all.at[me], b_send.at[d], b_recv.at[me], "replica", to)
        for d, to in enumerate(peers("replica"))
    ]
    for copy in b_out:
        copy.start()

    def a_right(j, k, src):
        return remote(src, a_all.at[j], a_send_r.at[k], a_recv.at[j], "replica", me + 1)

    def a_left(j, k, src):
        return remote(src, a_all.at[j], a_send_l.at[k], a_recv.at[j], "replica", me - 1)

    @pl.when(me < R - 1)
    def _():
        a_right(me, 0, a_hbm).start()

    @pl.when(me > 0)
    def _():
        a_left(me, 0, a_hbm).start()

    cnt_out = [
        remote(cnt_part.at[to], cnt_all.at[me], cnt_send.at[d], cnt_recv.at[me], "replica", to)
        for d, to in enumerate(peers("replica"))
    ]
    for copy in cnt_out:
        copy.start()
    cnt_all[me] = cnt_part[me]

    loads["b"].wait()
    loads["v"].wait()
    for to in peers("replica"):
        remote(b_hbm, b_all.at[to], b_send.at[0], b_recv.at[to], "replica", to).wait_recv()
    product = lax.dot_general(
        b_all[...].reshape(R * rows, vshare), v_own[...], (((1,), (1,)), ((), ())),
        preferred_element_type=F32,
    )
    cu = jnp.zeros((rank, tokens), F32)
    for s in range(adapters):
        cu = jnp.where(slot == s, product[s * rank:(s + 1) * rank, :], cu)
    cu_all[mt] = cu
    cu_out = [
        remote(cu_all.at[mt], cu_all.at[mt], cu_send.at[d], cu_recv.at[mt], "tensor", to)
        for d, to in enumerate(peers("tensor"))
    ]
    for copy in cu_out:
        copy.start()
    v_out = [
        remote(v_hbm, vcols(mt), v_send.at[d], v_recv.at[mt], "tensor", to)
        for d, to in enumerate(peers("tensor"))
    ]
    for copy in v_out:
        copy.start()

    def a_hop(k):
        @pl.when(me >= k)
        def _():
            j = me - k
            a_right(j, k, a_all.at[j]).wait_recv()
            if k < R - 1:
                @pl.when(me < R - 1)
                def _():
                    a_right(j, k, a_all.at[j]).start()

        @pl.when(me + k < R)
        def _():
            j = me + k
            a_left(j, k, a_all.at[j]).wait_recv()
            if k < R - 1:
                @pl.when(me > 0)
                def _():
                    a_left(j, k, a_all.at[j]).start()

    def add_cd(j):
        p = lax.dot_general(
            a_all[j], x[...], (((1,), (1,)), ((), ())), preferred_element_type=F32
        )
        acc = cd_all[mt]
        for s in range(owned):
            acc = jnp.where(slot == j * owned + s, p[s * rank:(s + 1) * rank, :], acc)
        cd_all[mt] = acc

    def cd_hop(k):
        @pl.when(me >= k)
        def _():
            add_cd(me - k)

        @pl.when(me + k < R)
        def _():
            add_cd(me + k)

    loads["a"].wait()
    loads["x"].wait()
    a_hop(1)

    for to in peers("tensor"):
        remote(cu_all.at[to], cu_all.at[to], cu_send.at[0], cu_recv.at[to], "tensor", to).wait_recv()
    c = cu_all[0]
    for q in range(1, T):
        c = c + cu_all[q]
    c = c.astype(BF16).astype(F32)
    spread = jnp.concatenate([jnp.where(slot == s, c, 0.0) for s in range(adapters)], axis=0)
    cm[...] = spread.astype(BF16).reshape(R, rows, tokens)

    def rs_right(d):
        return remote(snd.at[d], hop_r.at[d], rs_send.at[d], rs_recv_r.at[d], "replica", me + 1)

    def rs_left(d):
        return remote(snd.at[d], hop_l.at[d], rs_send.at[d], rs_recv_l.at[d], "replica", me - 1)

    order = []
    for i in range((R + 1) // 2):
        order += [R - 1 - i] + ([i] if i != R - 1 - i else [])
    for j in order:
        p = jnp.dot(cm[j], x[...], preferred_element_type=F32)
        part[j] = p
        if j > 0:
            @pl.when(me == 0)
            def _():
                snd[j] = part[j].astype(BF16)
                rs_right(j).start()
        if j < R - 1:
            @pl.when(me == R - 1)
            def _():
                snd[j] = part[j].astype(BF16)
                rs_left(j).start()

    def relay(k):
        d = R - 1 - k

        @pl.when((me > 0) & (me < d))
        def _():
            rs_right(d).wait_recv()
            snd[d] = (part[d] + hop_r[d].astype(F32)).astype(BF16)
            rs_right(d).start()

        @pl.when((me < R - 1) & (me > k))
        def _():
            rs_left(k).wait_recv()
            snd[k] = (part[k] + hop_l[k].astype(F32)).astype(BF16)
            rs_left(k).start()

    cd_all[mt] = jnp.zeros((rank, tokens), F32)
    add_cd(me)
    a_hop(2)
    cd_hop(1)
    relay(0)
    cmt[...] = spread.T.astype(BF16)
    cd_hop(2)
    for k in range(3, R):
        a_hop(k)
        cd_hop(k)
    cd_out = [
        remote(cd_all.at[mt], cd_all.at[mt], cd_send.at[d], cd_recv.at[mt], "tensor", to)
        for d, to in enumerate(peers("tensor"))
    ]
    for copy in cd_out:
        copy.start()
    for k in range(1, R - 1):
        relay(k)

    for to in peers("tensor"):
        remote(cd_all.at[to], cd_all.at[to], cd_send.at[0], cd_recv.at[to], "tensor", to).wait_recv()
    c = cd_all[0]
    for q in range(1, T):
        c = c + cd_all[q]
    c = c.astype(BF16).astype(F32)
    spread = jnp.concatenate([jnp.where(slot == s, c, 0.0) for s in range(adapters)], axis=0)
    up_part[...] = jnp.dot(
        spread.astype(BF16), v_own[...], preferred_element_type=F32
    ).reshape(R, rows, vshare)
    up_out = [
        remote(up_part.at[to], up_all.at[me], up_send.at[d], up_recv.at[me], "replica", to)
        for d, to in enumerate(peers("replica"))
    ]
    for copy in up_out:
        copy.start()
    up_all[me] = up_part[me]

    loads["vf"].wait()
    loads["w"].wait()
    for to in peers("tensor"):
        remote(v_hbm, vcols(to), v_send.at[0], v_recv.at[to], "tensor", to).wait_recv()
    tile = 256 if width % 256 == 0 else 128

    @pl.loop(0, width // tile)
    def _(i):
        at = pl.ds(pl.multiple_of(i * tile, tile), tile)
        lora = jnp.dot(
            cmt[...], a_all[:, :, at].reshape(R * rows, tile), preferred_element_type=F32
        ).astype(BF16).astype(F32)
        base = lax.dot_general(
            v_full[...], w[at, :], (((1,), (1,)), ((), ())), preferred_element_type=F32
        )
        hid[:, at] = (base + SCALING * lora).astype(BF16)

    hid_out = pltpu.make_async_copy(hid, hid_hbm, load_sem.at[6])
    hid_out.start()

    for to in peers("replica"):
        remote(cnt_part.at[to], cnt_all.at[to], cnt_send.at[0], cnt_recv.at[to], "replica", to).wait_recv()
    count = cnt_all[0]
    for j in range(1, R):
        count = count + cnt_all[j]
    count = jnp.where(lax.broadcasted_iota(jnp.int32, count.shape, 0) < owned, count, 1.0)
    factor = SCALING / count

    @pl.when(me > 0)
    def _():
        rs_right(me).wait_recv()
        part[me] = part[me] + hop_r[me].astype(F32)

    @pl.when(me < R - 1)
    def _():
        rs_left(me).wait_recv()
        part[me] = part[me] + hop_l[me].astype(F32)

    for s in range(owned):
        at = pl.ds(s * rank, rank)
        down_ref[at, :] = (part[me, at, :] * factor[s:s + 1, 0:1]).astype(BF16)

    for to in peers("replica"):
        remote(up_part.at[to], up_all.at[to], up_send.at[0], up_recv.at[to], "replica", to).wait_recv()
    total = up_all[0]
    for j in range(1, R):
        total = total + up_all[j]
    for s in range(owned):
        at = slice(s * rank, (s + 1) * rank)
        up_ref[at, :] = (total[at, :] * factor[s:s + 1, 0:1]).astype(BF16)

    for copy in b_out + cnt_out + cu_out + v_out + cd_out + up_out:
        copy.wait_send()
    for k in range(R - 1):
        @pl.when((me >= k) & (me < R - 1))
        def _():
            a_right(me - k, k, a_all.at[me - k]).wait_send()

        @pl.when((me + k < R) & (me > 0))
        def _():
            a_left(me + k, k, a_all.at[me + k]).wait_send()
    for d in range(R):
        @pl.when(me < d)
        def _():
            rs_right(d).wait_send()

        @pl.when(me > d)
        def _():
            rs_left(d).wait_send()
    hid_out.wait()


def scratch_of(R, T, owned, rank, tokens, width, vshare):
    rows = owned * rank
    features = T * vshare
    pad = -(-owned // 8) * 8
    buffers = [
        ((tokens, width), BF16),
        ((width, features), BF16),
        ((tokens, vshare), BF16),
        ((tokens, features), BF16),
        ((R, rows, width), BF16),
        ((R, rows, vshare), BF16),
        ((tokens, width), BF16),
        ((T, rank, tokens), F32),
        ((T, rank, tokens), F32),
        ((R, rows, tokens), BF16),
        ((tokens, R * rows), BF16),
        ((R, rows, width), F32),
        ((R, rows, width), BF16),
        ((R, rows, width), BF16),
        ((R, rows, width), BF16),
        ((R, rows, vshare), F32),
        ((R, rows, vshare), F32),
        ((R, pad, 128), F32),
        ((R, pad, 128), F32),
    ]
    sems = [7] + [R] * 6 + [R, R, T, T, T, T, T, T, R, R, R, R]
    size = sum(math.prod(shape) * jnp.dtype(kind).itemsize for shape, kind in buffers)
    return size, [pltpu.VMEM(*b) for b in buffers] + [pltpu.SemaphoreType.DMA((n,)) for n in sems]


VMEM_LIMIT = 40 * 1024 * 1024


def shards(
    hidden_input_saved,
    value_output_gradient,
    frozen_value_weight,
    adapter_lower_factor,
    adapter_upper_factor,
    per_token_adapter,
    adapter_table_slot,
):
    R, T = lax.axis_size("replica"), lax.axis_size("tensor")
    owned, rank, width = adapter_lower_factor.shape
    vshare = adapter_upper_factor.shape[2]
    tokens = hidden_input_saved.shape[0]
    size, scratch = scratch_of(R, T, owned, rank, tokens, width, vshare)
    if size > VMEM_LIMIT // 2:
        return dispatched(
            hidden_input_saved, value_output_gradient, frozen_value_weight,
            adapter_lower_factor, adapter_upper_factor, per_token_adapter, adapter_table_slot,
        )
    rows = owned * rank
    anywhere = pl.BlockSpec(memory_space=pl.ANY)
    vmem = pl.BlockSpec(memory_space=pltpu.VMEM)
    hidden_grad, down_grad, up_grad = pl.pallas_call(
        functools.partial(fused_body, R, T, owned),
        out_shape=(
            jax.ShapeDtypeStruct((tokens, width), BF16),
            jax.ShapeDtypeStruct((rows, width), BF16),
            jax.ShapeDtypeStruct((rows, vshare), BF16),
        ),
        in_specs=[anywhere] * 5 + [vmem, pl.BlockSpec(memory_space=pltpu.SMEM)],
        out_specs=(anywhere, vmem, vmem),
        scratch_shapes=scratch,
        compiler_params=pltpu.CompilerParams(
            collective_id=0, has_side_effects=True, vmem_limit_bytes=VMEM_LIMIT
        ),
        name="lora_value_backward",
    )(
        hidden_input_saved,
        value_output_gradient,
        frozen_value_weight,
        adapter_lower_factor.reshape(rows, width),
        adapter_upper_factor.reshape(rows, vshare),
        per_token_adapter.reshape(1, tokens),
        adapter_table_slot,
    )
    return (
        hidden_grad,
        down_grad.reshape(owned, rank, width),
        up_grad.reshape(owned, rank, vshare),
    )


def dispatched(
    hidden_input_saved,
    value_output_gradient,
    frozen_value_weight,
    adapter_lower_factor,
    adapter_upper_factor,
    per_token_adapter,
    adapter_table_slot,
):
    replicas = lax.axis_size("replica")
    local_owned_count, reduced_rank_product, share_width = adapter_lower_factor.shape
    value_head_share = adapter_upper_factor.shape[2]
    tokens_here = hidden_input_saved.shape[0]
    adapters = local_owned_count * replicas
    capacity = max(2, 3 * tokens_here // adapters)
    slot_total_count = adapters * capacity
    full_grad = lax.all_gather(value_output_gradient, "tensor", axis=1, tiled=True)
    base_grad = lax.dot_general(
        full_grad, frozen_value_weight, (((1,), (1,)), ((), ())), preferred_element_type=jnp.float32
    )
    adapter_ids = per_token_adapter[:, 0]
    catalog = jnp.arange(adapters, dtype=jnp.int32)
    slot_ids = jnp.sum(
        jnp.where(adapter_ids[:, None] == catalog[None, :], adapter_table_slot[None, :], 0), axis=1
    )
    one_hot = (slot_ids[:, None] == catalog[None, :]).astype(jnp.int32)
    position = jnp.sum(one_hot * jnp.cumsum(one_hot, axis=0), axis=1) - 1
    destination_index = slot_ids * capacity + position
    rows_send = (
        jnp.zeros((slot_total_count, share_width), jnp.bfloat16)
        .at[destination_index]
        .set(hidden_input_saved)
    )
    value_send = (
        jnp.zeros((slot_total_count, value_head_share), jnp.bfloat16)
        .at[destination_index]
        .set(value_output_gradient)
    )
    marks_send = (
        jnp.zeros((slot_total_count,), jnp.bfloat16)
        .at[destination_index]
        .set(jnp.ones((tokens_here,), jnp.bfloat16))
    )
    incoming_rows, value_input_rows, marks_in = (
        lax.all_to_all(
            rows_send.reshape(replicas, local_owned_count, capacity, share_width),
            "replica",
            split_axis=0,
            concat_axis=0,
            tiled=True,
        ),
        lax.all_to_all(
            value_send.reshape(replicas, local_owned_count, capacity, value_head_share),
            "replica",
            split_axis=0,
            concat_axis=0,
            tiled=True,
        ),
        lax.all_to_all(
            marks_send.reshape(replicas, local_owned_count, capacity),
            "replica",
            split_axis=0,
            concat_axis=0,
            tiled=True,
        ),
    )
    lower_factor_share = jnp.einsum(
        "woip,osp->oswi", incoming_rows, adapter_lower_factor, preferred_element_type=jnp.float32
    )
    upper_factor_share = jnp.einsum(
        "xluq,liq->lixu", value_input_rows, adapter_upper_factor, preferred_element_type=jnp.float32
    )
    flat_shape = (local_owned_count, reduced_rank_product, replicas * capacity)
    down_sum, up_sum = lax.psum(
        (lower_factor_share.reshape(flat_shape), upper_factor_share.reshape(flat_shape)), "tensor"
    )
    coeff_down = down_sum.reshape(lower_factor_share.shape).astype(jnp.bfloat16)
    upper_coefficient = up_sum.reshape(upper_factor_share.shape).astype(jnp.bfloat16)
    counts = jnp.sum(marks_in.astype(jnp.float32), axis=(0, 2))
    factor = SCALING / counts
    down_grad = (
        jnp.einsum(
            "arnc,nacd->ard", upper_coefficient, incoming_rows, preferred_element_type=jnp.float32
        )
        * factor[:, None, None]
    ).astype(jnp.bfloat16)
    up_grad = (
        jnp.einsum(
            "arnc,nace->are", coeff_down, value_input_rows, preferred_element_type=jnp.float32
        )
        * factor[:, None, None]
    ).astype(jnp.bfloat16)
    coeff_send = jnp.transpose(upper_coefficient, (2, 0, 3, 1))
    coeff_back = lax.all_to_all(
        coeff_send, "replica", split_axis=0, concat_axis=0, tiled=True
    ).reshape(adapters, capacity, reduced_rank_product)
    adapter_token_rows = (
        jnp.einsum(
            "acr,ard->acd",
            coeff_back,
            lax.all_gather(adapter_lower_factor, "replica", axis=0, tiled=True),
            preferred_element_type=jnp.float32,
        )
        .astype(jnp.bfloat16)
        .reshape(slot_total_count, share_width)
    )
    selected_rows = adapter_token_rows[destination_index]
    hidden_grad = (base_grad + SCALING * selected_rows.astype(jnp.float32)).astype(jnp.bfloat16)
    return (hidden_grad, down_grad, up_grad)


def solution(mesh):
    placed = (
        P(("groups", "replica"), "tensor"),
        P(("groups", "replica"), "tensor"),
        P("tensor", None),
        P(("groups", "replica"), None, "tensor"),
        P(("groups", "replica"), None, "tensor"),
        P(("groups", "replica"), None),
        P("groups"),
    )
    return jax.shard_map(
        shards,
        mesh=mesh,
        in_specs=placed,
        out_specs=(
            P(("groups", "replica"), "tensor"),
            P(("groups", "replica"), None, "tensor"),
            P(("groups", "replica"), None, "tensor"),
        ),
        check_vma=False,
    )
```

```python
import functools
import math

import jax
import jax.numpy as jnp
from jax import lax
from jax.experimental import pallas as pl
from jax.experimental.pallas import tpu as pltpu
from jax.sharding import PartitionSpec as P

SCALING = 2.0

MESH = pl.DeviceIdType.MESH
F32 = jnp.float32
BF16 = jnp.bfloat16


def fused_body(
    replicas,
    tensors,
    owned,
    x_hbm,
    v_hbm,
    w_hbm,
    a_hbm,
    b_hbm,
    ids_hbm,
    table_hbm,
    hid,
    down_ref,
    up_ref,
    x,
    w,
    v_own,
    v_full,
    a_all,
    b_all,
    cu_all,
    cd_all,
    cm,
    cmt,
    part,
    snd,
    hop,
    up_part,
    up_all,
    cnt_part,
    cnt_all,
    ids_ref,
    table_ref,
    load_sem,
    a_send_r,
    a_send_l,
    a_recv,
    rs_send,
    rs_recv,
    b_send,
    b_recv,
    v_send,
    v_recv,
    cu_send,
    cu_recv,
    cd_send,
    cd_recv,
    up_send,
    up_recv,
    cnt_send,
    cnt_recv,
):
    R, T = replicas, tensors
    me = lax.axis_index("replica")
    mt = lax.axis_index("tensor")
    rows = a_hbm.shape[0]
    rank = rows // owned
    tokens, width = x_hbm.shape
    vshare = v_hbm.shape[1]
    adapters = R * owned

    def remote(src, dst, send, recv, axis, to):
        return pltpu.make_async_remote_copy(
            src_ref=src, dst_ref=dst, send_sem=send, recv_sem=recv,
            device_id={axis: to}, device_id_type=MESH,
        )

    def peers(axis):
        n, here = (R, me) if axis == "replica" else (T, mt)
        return [lax.rem(here + d, n) for d in range(1, n)]

    def vcols(i):
        return v_full.at[:, pl.ds(pl.multiple_of(i * vshare, vshare), vshare)]

    loads = {
        "ids": pltpu.make_async_copy(ids_hbm, ids_ref, load_sem.at[7]),
        "table": pltpu.make_async_copy(table_hbm, table_ref, load_sem.at[8]),
        "b": pltpu.make_async_copy(b_hbm, b_all.at[me], load_sem.at[0]),
        "v": pltpu.make_async_copy(v_hbm, v_own, load_sem.at[1]),
        "x": pltpu.make_async_copy(x_hbm, x, load_sem.at[2]),
        "a": pltpu.make_async_copy(a_hbm, a_all.at[me], load_sem.at[3]),
        "vf": pltpu.make_async_copy(v_hbm, vcols(mt), load_sem.at[4]),
        "w": pltpu.make_async_copy(w_hbm, w, load_sem.at[5]),
    }
    for name in ("ids", "table", "b", "v", "x", "a", "vf", "w"):
        loads[name].start()

    barrier = pltpu.get_barrier_semaphore()
    for axis in ("replica", "tensor"):
        for to in peers(axis):
            pl.semaphore_signal(barrier, inc=1, device_id={axis: to}, device_id_type=MESH)

    loads["ids"].wait()
    loads["table"].wait()
    ids = ids_ref[...]
    slot = jnp.zeros_like(ids)
    for i in range(adapters):
        slot = jnp.where(ids == i, table_ref[i], slot)
    slot = jnp.broadcast_to(slot, (rank, tokens))
    pad = cnt_part.shape[1]
    for j in range(R):
        which = lax.broadcasted_iota(jnp.int32, (pad, tokens), 0)
        hit = (slot[0:pad, :] == which + j * owned) & (which < owned)
        total = jnp.sum(hit.astype(F32), axis=1, keepdims=True)
        cnt_part[j] = jnp.broadcast_to(total, (pad, 128))

    pl.semaphore_wait(barrier, R - 1 + T - 1)

    b_out = [
        remote(b_hbm, b_all.at[me], b_send.at[d], b_recv.at[me], "replica", to)
        for d, to in enumerate(peers("replica"))
    ]
    for copy in b_out:
        copy.start()

    def a_right(j, k, src):
        return remote(src, a_all.at[j], a_send_r.at[k], a_recv.at[j], "replica", me + 1)

    def a_left(j, k, src):
        return remote(src, a_all.at[j], a_send_l.at[k], a_recv.at[j], "replica", me - 1)

    @pl.when(me < R - 1)
    def _():
        a_right(me, 0, a_hbm).start()

    @pl.when(me > 0)
    def _():
        a_left(me, 0, a_hbm).start()

    cnt_out = [
        remote(cnt_part.at[to], cnt_all.at[me], cnt_send.at[d], cnt_recv.at[me], "replica", to)
        for d, to in enumerate(peers("replica"))
    ]
    for copy in cnt_out:
        copy.start()
    cnt_all[me] = cnt_part[me]

    loads["b"].wait()
    loads["v"].wait()
    for to in peers("replica"):
        remote(b_hbm, b_all.at[to], b_send.at[0], b_recv.at[to], "replica", to).wait_recv()
    product = lax.dot_general(
        b_all[...].reshape(R * rows, vshare), v_own[...], (((1,), (1,)), ((), ())),
        preferred_element_type=F32,
    )
    cu = jnp.zeros((rank, tokens), F32)
    for s in range(adapters):
        cu = jnp.where(slot == s, product[s * rank:(s + 1) * rank, :], cu)
    cu_all[mt] = cu
    cu_out = [
        remote(cu_all.at[mt], cu_all.at[mt], cu_send.at[d], cu_recv.at[mt], "tensor", to)
        for d, to in enumerate(peers("tensor"))
    ]
    for copy in cu_out:
        copy.start()
    v_out = [
        remote(v_hbm, vcols(mt), v_send.at[d], v_recv.at[mt], "tensor", to)
        for d, to in enumerate(peers("tensor"))
    ]
    for copy in v_out:
        copy.start()

    def a_hop(k):
        @pl.when(me >= k)
        def _():
            j = me - k
            a_right(j, k, a_all.at[j]).wait_recv()
            if k < R - 1:
                @pl.when(me < R - 1)
                def _():
                    a_right(j, k, a_all.at[j]).start()

        @pl.when(me + k < R)
        def _():
            j = me + k
            a_left(j, k, a_all.at[j]).wait_recv()
            if k < R - 1:
                @pl.when(me > 0)
                def _():
                    a_left(j, k, a_all.at[j]).start()

    def add_cd(j):
        p = lax.dot_general(
            a_all[j], x[...], (((1,), (1,)), ((), ())), preferred_element_type=F32
        )
        acc = cd_all[mt]
        for s in range(owned):
            acc = jnp.where(slot == j * owned + s, p[s * rank:(s + 1) * rank, :], acc)
        cd_all[mt] = acc

    def cd_hop(k):
        @pl.when(me >= k)
        def _():
            add_cd(me - k)

        @pl.when(me + k < R)
        def _():
            add_cd(me + k)

    loads["a"].wait()
    loads["x"].wait()
    a_hop(1)

    for to in peers("tensor"):
        remote(cu_all.at[to], cu_all.at[to], cu_send.at[0], cu_recv.at[to], "tensor", to).wait_recv()
    c = cu_all[0]
    for q in range(1, T):
        c = c + cu_all[q]
    c = c.astype(BF16).astype(F32)
    spread = jnp.concatenate([jnp.where(slot == s, c, 0.0) for s in range(adapters)], axis=0)
    cm[...] = spread.astype(BF16).reshape(R, rows, tokens)

    def rs_to(d):
        return remote(snd.at[d], hop.at[me], rs_send.at[d], rs_recv.at[me], "replica", d)

    order = []
    for i in range((R + 1) // 2):
        order += [R - 1 - i] + ([i] if i != R - 1 - i else [])
    for j in order:
        p = jnp.dot(cm[j], x[...], preferred_element_type=F32)

        @pl.when(me == j)
        def _():
            part[...] = p

        @pl.when(me != j)
        def _():
            snd[j] = p.astype(BF16)
            rs_to(j).start()

    cd_all[mt] = jnp.zeros((rank, tokens), F32)
    add_cd(me)
    a_hop(2)
    cd_hop(1)
    cmt[...] = spread.T.astype(BF16)
    cd_hop(2)
    for k in range(3, R):
        a_hop(k)
        cd_hop(k)
    cd_out = [
        remote(cd_all.at[mt], cd_all.at[mt], cd_send.at[d], cd_recv.at[mt], "tensor", to)
        for d, to in enumerate(peers("tensor"))
    ]
    for copy in cd_out:
        copy.start()

    for to in peers("tensor"):
        remote(cd_all.at[to], cd_all.at[to], cd_send.at[0], cd_recv.at[to], "tensor", to).wait_recv()
    c = cd_all[0]
    for q in range(1, T):
        c = c + cd_all[q]
    c = c.astype(BF16).astype(F32)
    spread = jnp.concatenate([jnp.where(slot == s, c, 0.0) for s in range(adapters)], axis=0)
    up_part[...] = jnp.dot(
        spread.astype(BF16), v_own[...], preferred_element_type=F32
    ).reshape(R, rows, vshare)
    up_out = [
        remote(up_part.at[to], up_all.at[me], up_send.at[d], up_recv.at[me], "replica", to)
        for d, to in enumerate(peers("replica"))
    ]
    for copy in up_out:
        copy.start()
    up_all[me] = up_part[me]

    loads["vf"].wait()
    loads["w"].wait()
    for to in peers("tensor"):
        remote(v_hbm, vcols(to), v_send.at[0], v_recv.at[to], "tensor", to).wait_recv()
    tile = 256 if width % 256 == 0 else 128

    @pl.loop(0, width // tile)
    def _(i):
        at = pl.ds(pl.multiple_of(i * tile, tile), tile)
        lora = jnp.dot(
            cmt[...], a_all[:, :, at].reshape(R * rows, tile), preferred_element_type=F32
        ).astype(BF16).astype(F32)
        base = lax.dot_general(
            v_full[...], w[at, :], (((1,), (1,)), ((), ())), preferred_element_type=F32
        )
        hid[:, at] = (base + SCALING * lora).astype(BF16)

    for to in peers("replica"):
        remote(cnt_part.at[to], cnt_all.at[to], cnt_send.at[0], cnt_recv.at[to], "replica", to).wait_recv()
    count = cnt_all[0]
    for j in range(1, R):
        count = count + cnt_all[j]
    count = jnp.where(lax.broadcasted_iota(jnp.int32, count.shape, 0) < owned, count, 1.0)
    factor = SCALING / count

    for to in peers("replica"):
        remote(snd.at[to], hop.at[to], rs_send.at[0], rs_recv.at[to], "replica", to).wait_recv()
        part[...] = part[...] + hop[to].astype(F32)

    for s in range(owned):
        at = pl.ds(s * rank, rank)
        down_ref[at, :] = (part[at, :] * factor[s:s + 1, 0:1]).astype(BF16)

    for to in peers("replica"):
        remote(up_part.at[to], up_all.at[to], up_send.at[0], up_recv.at[to], "replica", to).wait_recv()
    total = up_all[0]
    for j in range(1, R):
        total = total + up_all[j]
    for s in range(owned):
        at = slice(s * rank, (s + 1) * rank)
        up_ref[at, :] = (total[at, :] * factor[s:s + 1, 0:1]).astype(BF16)

    for copy in b_out + cnt_out + cu_out + v_out + cd_out + up_out:
        copy.wait_send()
    for k in range(R - 1):
        @pl.when((me >= k) & (me < R - 1))
        def _():
            a_right(me - k, k, a_all.at[me - k]).wait_send()

        @pl.when((me + k < R) & (me > 0))
        def _():
            a_left(me + k, k, a_all.at[me + k]).wait_send()
    for d in range(R):
        @pl.when(me != d)
        def _():
            rs_to(d).wait_send()


def scratch_of(R, T, owned, rank, tokens, width, vshare):
    rows = owned * rank
    features = T * vshare
    pad = -(-owned // 8) * 8
    buffers = [
        ((tokens, width), BF16),
        ((width, features), BF16),
        ((tokens, vshare), BF16),
        ((tokens, features), BF16),
        ((R, rows, width), BF16),
        ((R, rows, vshare), BF16),
        ((T, rank, tokens), F32),
        ((T, rank, tokens), F32),
        ((R, rows, tokens), BF16),
        ((tokens, R * rows), BF16),
        ((rows, width), F32),
        ((R, rows, width), BF16),
        ((R, rows, width), BF16),
        ((R, rows, vshare), F32),
        ((R, rows, vshare), F32),
        ((R, pad, 128), F32),
        ((R, pad, 128), F32),
    ]
    sems = [9] + [R] * 5 + [R, R, T, T, T, T, T, T, R, R, R, R]
    size = sum(math.prod(shape) * jnp.dtype(kind).itemsize for shape, kind in buffers)
    small = [pltpu.VMEM((1, tokens), jnp.int32), pltpu.SMEM((R * owned,), jnp.int32)]
    return size, [pltpu.VMEM(*b) for b in buffers] + small + [pltpu.SemaphoreType.DMA((n,)) for n in sems]


VMEM_LIMIT = 60 * 1024 * 1024


def shards(
    hidden_input_saved,
    value_output_gradient,
    frozen_value_weight,
    adapter_lower_factor,
    adapter_upper_factor,
    per_token_adapter,
    adapter_table_slot,
):
    R, T = lax.axis_size("replica"), lax.axis_size("tensor")
    owned, rank, width = adapter_lower_factor.shape
    vshare = adapter_upper_factor.shape[2]
    tokens = hidden_input_saved.shape[0]
    size, scratch = scratch_of(R, T, owned, rank, tokens, width, vshare)
    if size > VMEM_LIMIT // 3:
        return dispatched(
            hidden_input_saved, value_output_gradient, frozen_value_weight,
            adapter_lower_factor, adapter_upper_factor, per_token_adapter, adapter_table_slot,
        )
    rows = owned * rank
    anywhere = pl.BlockSpec(memory_space=pl.ANY)
    vmem = pl.BlockSpec(memory_space=pltpu.VMEM)
    hidden_grad, down_grad, up_grad = pl.pallas_call(
        functools.partial(fused_body, R, T, owned),
        out_shape=(
            pltpu.VMEM((tokens, width), BF16),
            jax.ShapeDtypeStruct((rows, width), BF16),
            jax.ShapeDtypeStruct((rows, vshare), BF16),
        ),
        in_specs=[pl.BlockSpec(memory_space=pltpu.HBM)] * 7,
        out_specs=(vmem, vmem, vmem),
        scratch_shapes=scratch,
        compiler_params=pltpu.CompilerParams(
            collective_id=0, has_side_effects=True, vmem_limit_bytes=VMEM_LIMIT
        ),
        name="lora_value_backward",
    )(
        hidden_input_saved,
        value_output_gradient,
        frozen_value_weight,
        adapter_lower_factor.reshape(rows, width),
        adapter_upper_factor.reshape(rows, vshare),
        per_token_adapter.reshape(1, tokens),
        adapter_table_slot,
    )
    return (
        hidden_grad,
        down_grad.reshape(owned, rank, width),
        up_grad.reshape(owned, rank, vshare),
    )


def dispatched(
    hidden_input_saved,
    value_output_gradient,
    frozen_value_weight,
    adapter_lower_factor,
    adapter_upper_factor,
    per_token_adapter,
    adapter_table_slot,
):
    replicas = lax.axis_size("replica")
    local_owned_count, reduced_rank_product, share_width = adapter_lower_factor.shape
    value_head_share = adapter_upper_factor.shape[2]
    tokens_here = hidden_input_saved.shape[0]
    adapters = local_owned_count * replicas
    capacity = max(2, 3 * tokens_here // adapters)
    slot_total_count = adapters * capacity
    full_grad = lax.all_gather(value_output_gradient, "tensor", axis=1, tiled=True)
    base_grad = lax.dot_general(
        full_grad, frozen_value_weight, (((1,), (1,)), ((), ())), preferred_element_type=jnp.float32
    )
    adapter_ids = per_token_adapter[:, 0]
    catalog = jnp.arange(adapters, dtype=jnp.int32)
    slot_ids = jnp.sum(
        jnp.where(adapter_ids[:, None] == catalog[None, :], adapter_table_slot[None, :], 0), axis=1
    )
    one_hot = (slot_ids[:, None] == catalog[None, :]).astype(jnp.int32)
    position = jnp.sum(one_hot * jnp.cumsum(one_hot, axis=0), axis=1) - 1
    destination_index = slot_ids * capacity + position
    rows_send = (
        jnp.zeros((slot_total_count, share_width), jnp.bfloat16)
        .at[destination_index]
        .set(hidden_input_saved)
    )
    value_send = (
        jnp.zeros((slot_total_count, value_head_share), jnp.bfloat16)
        .at[destination_index]
        .set(value_output_gradient)
    )
    marks_send = (
        jnp.zeros((slot_total_count,), jnp.bfloat16)
        .at[destination_index]
        .set(jnp.ones((tokens_here,), jnp.bfloat16))
    )
    incoming_rows, value_input_rows, marks_in = (
        lax.all_to_all(
            rows_send.reshape(replicas, local_owned_count, capacity, share_width),
            "replica",
            split_axis=0,
            concat_axis=0,
            tiled=True,
        ),
        lax.all_to_all(
            value_send.reshape(replicas, local_owned_count, capacity, value_head_share),
            "replica",
            split_axis=0,
            concat_axis=0,
            tiled=True,
        ),
        lax.all_to_all(
            marks_send.reshape(replicas, local_owned_count, capacity),
            "replica",
            split_axis=0,
            concat_axis=0,
            tiled=True,
        ),
    )
    lower_factor_share = jnp.einsum(
        "woip,osp->oswi", incoming_rows, adapter_lower_factor, preferred_element_type=jnp.float32
    )
    upper_factor_share = jnp.einsum(
        "xluq,liq->lixu", value_input_rows, adapter_upper_factor, preferred_element_type=jnp.float32
    )
    flat_shape = (local_owned_count, reduced_rank_product, replicas * capacity)
    down_sum, up_sum = lax.psum(
        (lower_factor_share.reshape(flat_shape), upper_factor_share.reshape(flat_shape)), "tensor"
    )
    coeff_down = down_sum.reshape(lower_factor_share.shape).astype(jnp.bfloat16)
    upper_coefficient = up_sum.reshape(upper_factor_share.shape).astype(jnp.bfloat16)
    counts = jnp.sum(marks_in.astype(jnp.float32), axis=(0, 2))
    factor = SCALING / counts
    down_grad = (
        jnp.einsum(
            "arnc,nacd->ard", upper_coefficient, incoming_rows, preferred_element_type=jnp.float32
        )
        * factor[:, None, None]
    ).astype(jnp.bfloat16)
    up_grad = (
        jnp.einsum(
            "arnc,nace->are", coeff_down, value_input_rows, preferred_element_type=jnp.float32
        )
        * factor[:, None, None]
    ).astype(jnp.bfloat16)
    coeff_send = jnp.transpose(upper_coefficient, (2, 0, 3, 1))
    coeff_back = lax.all_to_all(
        coeff_send, "replica", split_axis=0, concat_axis=0, tiled=True
    ).reshape(adapters, capacity, reduced_rank_product)
    adapter_token_rows = (
        jnp.einsum(
            "acr,ard->acd",
            coeff_back,
            lax.all_gather(adapter_lower_factor, "replica", axis=0, tiled=True),
            preferred_element_type=jnp.float32,
        )
        .astype(jnp.bfloat16)
        .reshape(slot_total_count, share_width)
    )
    selected_rows = adapter_token_rows[destination_index]
    hidden_grad = (base_grad + SCALING * selected_rows.astype(jnp.float32)).astype(jnp.bfloat16)
    return (hidden_grad, down_grad, up_grad)


def solution(mesh):
    placed = (
        P(("groups", "replica"), "tensor"),
        P(("groups", "replica"), "tensor"),
        P("tensor", None),
        P(("groups", "replica"), None, "tensor"),
        P(("groups", "replica"), None, "tensor"),
        P(("groups", "replica"), None),
        P("groups"),
    )
    return jax.shard_map(
        shards,
        mesh=mesh,
        in_specs=placed,
        out_specs=(
            P(("groups", "replica"), "tensor"),
            P(("groups", "replica"), None, "tensor"),
            P(("groups", "replica"), None, "tensor"),
        ),
        check_vma=False,
    )
```

```python
import functools
import math

import jax
import jax.numpy as jnp
from jax import lax
from jax.experimental import pallas as pl
from jax.experimental.pallas import tpu as pltpu
from jax.sharding import PartitionSpec as P

SCALING = 2.0

MESH = pl.DeviceIdType.MESH
F32 = jnp.float32
BF16 = jnp.bfloat16


def fused_body(
    replicas,
    tensors,
    owned,
    x_hbm,
    v_hbm,
    w_hbm,
    a_hbm,
    b_hbm,
    ids_hbm,
    table_hbm,
    hid,
    down_ref,
    up_ref,
    x,
    w,
    v_own,
    v_full,
    a_all,
    b_all,
    cu_all,
    cd_all,
    cm,
    cmt,
    part,
    snd,
    hop,
    hold,
    edge,
    up_part,
    up_all,
    cnt_part,
    cnt_all,
    ids_ref,
    table_ref,
    load_sem,
    a_send_r,
    a_send_l,
    a_recv,
    rs_send,
    rs_recv,
    edge_recv,
    b_send,
    b_recv,
    v_send,
    v_recv,
    cu_send,
    cu_recv,
    cd_send,
    cd_recv,
    up_send,
    up_recv,
    cnt_send,
    cnt_recv,
):
    R, T = replicas, tensors
    me = lax.axis_index("replica")
    mt = lax.axis_index("tensor")
    rows = a_hbm.shape[0]
    rank = rows // owned
    tokens, width = x_hbm.shape
    vshare = v_hbm.shape[1]
    adapters = R * owned

    def remote(src, dst, send, recv, axis, to):
        return pltpu.make_async_remote_copy(
            src_ref=src, dst_ref=dst, send_sem=send, recv_sem=recv,
            device_id={axis: to}, device_id_type=MESH,
        )

    def peers(axis):
        n, here = (R, me) if axis == "replica" else (T, mt)
        return [lax.rem(here + d, n) for d in range(1, n)]

    def vcols(i):
        return v_full.at[:, pl.ds(pl.multiple_of(i * vshare, vshare), vshare)]

    loads = {
        "ids": pltpu.make_async_copy(ids_hbm, ids_ref, load_sem.at[7]),
        "table": pltpu.make_async_copy(table_hbm, table_ref, load_sem.at[8]),
        "b": pltpu.make_async_copy(b_hbm, b_all.at[me], load_sem.at[0]),
        "v": pltpu.make_async_copy(v_hbm, v_own, load_sem.at[1]),
        "x": pltpu.make_async_copy(x_hbm, x, load_sem.at[2]),
        "a": pltpu.make_async_copy(a_hbm, a_all.at[me], load_sem.at[3]),
        "vf": pltpu.make_async_copy(v_hbm, vcols(mt), load_sem.at[4]),
        "w": pltpu.make_async_copy(w_hbm, w, load_sem.at[5]),
    }
    for name in ("ids", "table", "b", "v", "x", "a", "vf", "w"):
        loads[name].start()

    barrier = pltpu.get_barrier_semaphore()
    for axis in ("replica", "tensor"):
        for to in peers(axis):
            pl.semaphore_signal(barrier, inc=1, device_id={axis: to}, device_id_type=MESH)

    loads["ids"].wait()
    loads["table"].wait()
    ids = ids_ref[...]
    slot = jnp.zeros_like(ids)
    for i in range(adapters):
        slot = jnp.where(ids == i, table_ref[i], slot)
    slot = jnp.broadcast_to(slot, (rank, tokens))
    pad = cnt_part.shape[1]
    for j in range(R):
        which = lax.broadcasted_iota(jnp.int32, (pad, tokens), 0)
        hit = (slot[0:pad, :] == which + j * owned) & (which < owned)
        total = jnp.sum(hit.astype(F32), axis=1, keepdims=True)
        cnt_part[j] = jnp.broadcast_to(total, (pad, 128))

    pl.semaphore_wait(barrier, R - 1 + T - 1)

    b_out = [
        remote(b_hbm, b_all.at[me], b_send.at[d], b_recv.at[me], "replica", to)
        for d, to in enumerate(peers("replica"))
    ]
    for copy in b_out:
        copy.start()

    def a_right(j, k, src):
        return remote(src, a_all.at[j], a_send_r.at[k], a_recv.at[j], "replica", me + 1)

    def a_left(j, k, src):
        return remote(src, a_all.at[j], a_send_l.at[k], a_recv.at[j], "replica", me - 1)

    @pl.when(me < R - 1)
    def _():
        a_right(me, 0, a_hbm).start()

    @pl.when(me > 0)
    def _():
        a_left(me, 0, a_hbm).start()

    cnt_out = [
        remote(cnt_part.at[to], cnt_all.at[me], cnt_send.at[d], cnt_recv.at[me], "replica", to)
        for d, to in enumerate(peers("replica"))
    ]
    for copy in cnt_out:
        copy.start()
    cnt_all[me] = cnt_part[me]

    loads["b"].wait()
    loads["v"].wait()
    for to in peers("replica"):
        remote(b_hbm, b_all.at[to], b_send.at[0], b_recv.at[to], "replica", to).wait_recv()
    product = lax.dot_general(
        b_all[...].reshape(R * rows, vshare), v_own[...], (((1,), (1,)), ((), ())),
        preferred_element_type=F32,
    )
    cu = jnp.zeros((rank, tokens), F32)
    for s in range(adapters):
        cu = jnp.where(slot == s, product[s * rank:(s + 1) * rank, :], cu)
    cu_all[mt] = cu
    cu_out = [
        remote(cu_all.at[mt], cu_all.at[mt], cu_send.at[d], cu_recv.at[mt], "tensor", to)
        for d, to in enumerate(peers("tensor"))
    ]
    for copy in cu_out:
        copy.start()
    v_out = [
        remote(v_hbm, vcols(mt), v_send.at[d], v_recv.at[mt], "tensor", to)
        for d, to in enumerate(peers("tensor"))
    ]
    for copy in v_out:
        copy.start()

    def a_hop(k):
        @pl.when(me >= k)
        def _():
            j = me - k
            a_right(j, k, a_all.at[j]).wait_recv()
            if k < R - 1:
                @pl.when(me < R - 1)
                def _():
                    a_right(j, k, a_all.at[j]).start()

        @pl.when(me + k < R)
        def _():
            j = me + k
            a_left(j, k, a_all.at[j]).wait_recv()
            if k < R - 1:
                @pl.when(me > 0)
                def _():
                    a_left(j, k, a_all.at[j]).start()

    def add_cd(j):
        p = lax.dot_general(
            a_all[j], x[...], (((1,), (1,)), ((), ())), preferred_element_type=F32
        )
        acc = cd_all[mt]
        for s in range(owned):
            acc = jnp.where(slot == j * owned + s, p[s * rank:(s + 1) * rank, :], acc)
        cd_all[mt] = acc

    def cd_hop(k):
        @pl.when(me >= k)
        def _():
            add_cd(me - k)

        @pl.when(me + k < R)
        def _():
            add_cd(me + k)

    loads["a"].wait()
    loads["x"].wait()
    a_hop(1)

    for to in peers("tensor"):
        remote(cu_all.at[to], cu_all.at[to], cu_send.at[0], cu_recv.at[to], "tensor", to).wait_recv()
    c = cu_all[0]
    for q in range(1, T):
        c = c + cu_all[q]
    c = c.astype(BF16).astype(F32)
    spread = jnp.concatenate([jnp.where(slot == s, c, 0.0) for s in range(adapters)], axis=0)
    cm[...] = spread.astype(BF16).reshape(R, rows, tokens)

    def rs_to(d):
        return remote(snd.at[d], hop.at[me], rs_send.at[d], rs_recv.at[me], "replica", d)

    def to_next(d, to):
        return remote(snd.at[d], edge.at[d], rs_send.at[d], edge_recv.at[d], "replica", to)

    order = []
    for i in range((R + 1) // 2):
        order += [R - 1 - i] + ([i] if i != R - 1 - i else [])
    for j in order:
        p = jnp.dot(cm[j], x[...], preferred_element_type=F32)

        from_end = ((me == 1) & (j >= 2)) | ((me == R - 2) & (j <= R - 3))
        at_start = (me == 0) & (j >= 2)
        at_stop = (me == R - 1) & (j <= R - 3)

        @pl.when(me == j)
        def _():
            part[...] = p

        @pl.when(from_end)
        def _():
            hold[j] = p

        @pl.when((me != j) & jnp.logical_not(from_end))
        def _():
            snd[j] = p.astype(BF16)

        @pl.when(at_start)
        def _():
            to_next(j, me + 1).start()

        @pl.when(at_stop)
        def _():
            to_next(j, me - 1).start()

        @pl.when((me != j) & jnp.logical_not(from_end | at_start | at_stop))
        def _():
            rs_to(j).start()

    def pass_on(k):
        for mine, j in (((me == 1), R - 1 - k), ((me == R - 2), k)):
            @pl.when(mine)
            def _():
                to_next(j, me).wait_recv()
                snd[j] = (hold[j] + edge[j].astype(F32)).astype(BF16)
                rs_to(j).start()

    cd_all[mt] = jnp.zeros((rank, tokens), F32)
    add_cd(me)
    a_hop(2)
    cd_hop(1)
    if R > 2:
        pass_on(0)
    cmt[...] = spread.T.astype(BF16)
    cd_hop(2)
    for k in range(3, R):
        a_hop(k)
        cd_hop(k)
    cd_out = [
        remote(cd_all.at[mt], cd_all.at[mt], cd_send.at[d], cd_recv.at[mt], "tensor", to)
        for d, to in enumerate(peers("tensor"))
    ]
    for copy in cd_out:
        copy.start()

    for k in range(1, R - 2):
        pass_on(k)

    for to in peers("tensor"):
        remote(cd_all.at[to], cd_all.at[to], cd_send.at[0], cd_recv.at[to], "tensor", to).wait_recv()
    c = cd_all[0]
    for q in range(1, T):
        c = c + cd_all[q]
    c = c.astype(BF16).astype(F32)
    spread = jnp.concatenate([jnp.where(slot == s, c, 0.0) for s in range(adapters)], axis=0)
    up_part[...] = jnp.dot(
        spread.astype(BF16), v_own[...], preferred_element_type=F32
    ).reshape(R, rows, vshare)
    up_out = [
        remote(up_part.at[to], up_all.at[me], up_send.at[d], up_recv.at[me], "replica", to)
        for d, to in enumerate(peers("replica"))
    ]
    for copy in up_out:
        copy.start()
    up_all[me] = up_part[me]

    loads["vf"].wait()
    loads["w"].wait()
    for to in peers("tensor"):
        remote(v_hbm, vcols(to), v_send.at[0], v_recv.at[to], "tensor", to).wait_recv()
    tile = 256 if width % 256 == 0 else 128

    @pl.loop(0, width // tile)
    def _(i):
        at = pl.ds(pl.multiple_of(i * tile, tile), tile)
        lora = jnp.dot(
            cmt[...], a_all[:, :, at].reshape(R * rows, tile), preferred_element_type=F32
        ).astype(BF16).astype(F32)
        base = lax.dot_general(
            v_full[...], w[at, :], (((1,), (1,)), ((), ())), preferred_element_type=F32
        )
        hid[:, at] = (base + SCALING * lora).astype(BF16)

    for to in peers("replica"):
        remote(cnt_part.at[to], cnt_all.at[to], cnt_send.at[0], cnt_recv.at[to], "replica", to).wait_recv()
    count = cnt_all[0]
    for j in range(1, R):
        count = count + cnt_all[j]
    count = jnp.where(lax.broadcasted_iota(jnp.int32, count.shape, 0) < owned, count, 1.0)
    factor = SCALING / count

    for j in range(R):
        passed = ((me >= 2) & (j == 0)) | ((me <= R - 3) & (j == R - 1))

        @pl.when((me != j) & jnp.logical_not(passed))
        def _():
            remote(snd.at[j], hop.at[j], rs_send.at[0], rs_recv.at[j], "replica", j).wait_recv()
            part[...] = part[...] + hop[j].astype(F32)

    for s in range(owned):
        at = pl.ds(s * rank, rank)
        down_ref[at, :] = (part[at, :] * factor[s:s + 1, 0:1]).astype(BF16)

    for to in peers("replica"):
        remote(up_part.at[to], up_all.at[to], up_send.at[0], up_recv.at[to], "replica", to).wait_recv()
    total = up_all[0]
    for j in range(1, R):
        total = total + up_all[j]
    for s in range(owned):
        at = slice(s * rank, (s + 1) * rank)
        up_ref[at, :] = (total[at, :] * factor[s:s + 1, 0:1]).astype(BF16)

    for copy in b_out + cnt_out + cu_out + v_out + cd_out + up_out:
        copy.wait_send()
    for k in range(R - 1):
        @pl.when((me >= k) & (me < R - 1))
        def _():
            a_right(me - k, k, a_all.at[me - k]).wait_send()

        @pl.when((me + k < R) & (me > 0))
        def _():
            a_left(me + k, k, a_all.at[me + k]).wait_send()
    for d in range(R):
        @pl.when(me != d)
        def _():
            rs_to(d).wait_send()


def scratch_of(R, T, owned, rank, tokens, width, vshare):
    rows = owned * rank
    features = T * vshare
    pad = -(-owned // 8) * 8
    buffers = [
        ((tokens, width), BF16),
        ((width, features), BF16),
        ((tokens, vshare), BF16),
        ((tokens, features), BF16),
        ((R, rows, width), BF16),
        ((R, rows, vshare), BF16),
        ((T, rank, tokens), F32),
        ((T, rank, tokens), F32),
        ((R, rows, tokens), BF16),
        ((tokens, R * rows), BF16),
        ((rows, width), F32),
        ((R, rows, width), BF16),
        ((R, rows, width), BF16),
        ((R, rows, width), F32),
        ((R, rows, width), BF16),
        ((R, rows, vshare), F32),
        ((R, rows, vshare), F32),
        ((R, pad, 128), F32),
        ((R, pad, 128), F32),
    ]
    sems = [9] + [R] * 6 + [R, R, T, T, T, T, T, T, R, R, R, R]
    size = sum(math.prod(shape) * jnp.dtype(kind).itemsize for shape, kind in buffers)
    small = [pltpu.VMEM((1, tokens), jnp.int32), pltpu.SMEM((R * owned,), jnp.int32)]
    return size, [pltpu.VMEM(*b) for b in buffers] + small + [pltpu.SemaphoreType.DMA((n,)) for n in sems]


VMEM_LIMIT = 60 * 1024 * 1024


def shards(
    hidden_input_saved,
    value_output_gradient,
    frozen_value_weight,
    adapter_lower_factor,
    adapter_upper_factor,
    per_token_adapter,
    adapter_table_slot,
):
    R, T = lax.axis_size("replica"), lax.axis_size("tensor")
    owned, rank, width = adapter_lower_factor.shape
    vshare = adapter_upper_factor.shape[2]
    tokens = hidden_input_saved.shape[0]
    size, scratch = scratch_of(R, T, owned, rank, tokens, width, vshare)
    if size > VMEM_LIMIT // 3:
        return dispatched(
            hidden_input_saved, value_output_gradient, frozen_value_weight,
            adapter_lower_factor, adapter_upper_factor, per_token_adapter, adapter_table_slot,
        )
    rows = owned * rank
    anywhere = pl.BlockSpec(memory_space=pl.ANY)
    vmem = pl.BlockSpec(memory_space=pltpu.VMEM)
    hidden_grad, down_grad, up_grad = pl.pallas_call(
        functools.partial(fused_body, R, T, owned),
        out_shape=(
            pltpu.VMEM((tokens, width), BF16),
            jax.ShapeDtypeStruct((rows, width), BF16),
            jax.ShapeDtypeStruct((rows, vshare), BF16),
        ),
        in_specs=[pl.BlockSpec(memory_space=pltpu.HBM)] * 7,
        out_specs=(vmem, vmem, vmem),
        scratch_shapes=scratch,
        compiler_params=pltpu.CompilerParams(
            collective_id=0, has_side_effects=True, vmem_limit_bytes=VMEM_LIMIT
        ),
        name="lora_value_backward",
    )(
        hidden_input_saved,
        value_output_gradient,
        frozen_value_weight,
        adapter_lower_factor.reshape(rows, width),
        adapter_upper_factor.reshape(rows, vshare),
        per_token_adapter.reshape(1, tokens),
        adapter_table_slot,
    )
    return (
        hidden_grad,
        down_grad.reshape(owned, rank, width),
        up_grad.reshape(owned, rank, vshare),
    )


def dispatched(
    hidden_input_saved,
    value_output_gradient,
    frozen_value_weight,
    adapter_lower_factor,
    adapter_upper_factor,
    per_token_adapter,
    adapter_table_slot,
):
    replicas = lax.axis_size("replica")
    local_owned_count, reduced_rank_product, share_width = adapter_lower_factor.shape
    value_head_share = adapter_upper_factor.shape[2]
    tokens_here = hidden_input_saved.shape[0]
    adapters = local_owned_count * replicas
    capacity = max(2, 3 * tokens_here // adapters)
    slot_total_count = adapters * capacity
    full_grad = lax.all_gather(value_output_gradient, "tensor", axis=1, tiled=True)
    base_grad = lax.dot_general(
        full_grad, frozen_value_weight, (((1,), (1,)), ((), ())), preferred_element_type=jnp.float32
    )
    adapter_ids = per_token_adapter[:, 0]
    catalog = jnp.arange(adapters, dtype=jnp.int32)
    slot_ids = jnp.sum(
        jnp.where(adapter_ids[:, None] == catalog[None, :], adapter_table_slot[None, :], 0), axis=1
    )
    one_hot = (slot_ids[:, None] == catalog[None, :]).astype(jnp.int32)
    position = jnp.sum(one_hot * jnp.cumsum(one_hot, axis=0), axis=1) - 1
    destination_index = slot_ids * capacity + position
    rows_send = (
        jnp.zeros((slot_total_count, share_width), jnp.bfloat16)
        .at[destination_index]
        .set(hidden_input_saved)
    )
    value_send = (
        jnp.zeros((slot_total_count, value_head_share), jnp.bfloat16)
        .at[destination_index]
        .set(value_output_gradient)
    )
    marks_send = (
        jnp.zeros((slot_total_count,), jnp.bfloat16)
        .at[destination_index]
        .set(jnp.ones((tokens_here,), jnp.bfloat16))
    )
    incoming_rows, value_input_rows, marks_in = (
        lax.all_to_all(
            rows_send.reshape(replicas, local_owned_count, capacity, share_width),
            "replica",
            split_axis=0,
            concat_axis=0,
            tiled=True,
        ),
        lax.all_to_all(
            value_send.reshape(replicas, local_owned_count, capacity, value_head_share),
            "replica",
            split_axis=0,
            concat_axis=0,
            tiled=True,
        ),
        lax.all_to_all(
            marks_send.reshape(replicas, local_owned_count, capacity),
            "replica",
            split_axis=0,
            concat_axis=0,
            tiled=True,
        ),
    )
    lower_factor_share = jnp.einsum(
        "woip,osp->oswi", incoming_rows, adapter_lower_factor, preferred_element_type=jnp.float32
    )
    upper_factor_share = jnp.einsum(
        "xluq,liq->lixu", value_input_rows, adapter_upper_factor, preferred_element_type=jnp.float32
    )
    flat_shape = (local_owned_count, reduced_rank_product, replicas * capacity)
    down_sum, up_sum = lax.psum(
        (lower_factor_share.reshape(flat_shape), upper_factor_share.reshape(flat_shape)), "tensor"
    )
    coeff_down = down_sum.reshape(lower_factor_share.shape).astype(jnp.bfloat16)
    upper_coefficient = up_sum.reshape(upper_factor_share.shape).astype(jnp.bfloat16)
    counts = jnp.sum(marks_in.astype(jnp.float32), axis=(0, 2))
    factor = SCALING / counts
    down_grad = (
        jnp.einsum(
            "arnc,nacd->ard", upper_coefficient, incoming_rows, preferred_element_type=jnp.float32
        )
        * factor[:, None, None]
    ).astype(jnp.bfloat16)
    up_grad = (
        jnp.einsum(
            "arnc,nace->are", coeff_down, value_input_rows, preferred_element_type=jnp.float32
        )
        * factor[:, None, None]
    ).astype(jnp.bfloat16)
    coeff_send = jnp.transpose(upper_coefficient, (2, 0, 3, 1))
    coeff_back = lax.all_to_all(
        coeff_send, "replica", split_axis=0, concat_axis=0, tiled=True
    ).reshape(adapters, capacity, reduced_rank_product)
    adapter_token_rows = (
        jnp.einsum(
            "acr,ard->acd",
            coeff_back,
            lax.all_gather(adapter_lower_factor, "replica", axis=0, tiled=True),
            preferred_element_type=jnp.float32,
        )
        .astype(jnp.bfloat16)
        .reshape(slot_total_count, share_width)
    )
    selected_rows = adapter_token_rows[destination_index]
    hidden_grad = (base_grad + SCALING * selected_rows.astype(jnp.float32)).astype(jnp.bfloat16)
    return (hidden_grad, down_grad, up_grad)


def solution(mesh):
    placed = (
        P(("groups", "replica"), "tensor"),
        P(("groups", "replica"), "tensor"),
        P("tensor", None),
        P(("groups", "replica"), None, "tensor"),
        P(("groups", "replica"), None, "tensor"),
        P(("groups", "replica"), None),
        P("groups"),
    )
    return jax.shard_map(
        shards,
        mesh=mesh,
        in_specs=placed,
        out_specs=(
            P(("groups", "replica"), "tensor"),
            P(("groups", "replica"), None, "tensor"),
            P(("groups", "replica"), None, "tensor"),
        ),
        check_vma=False,
    )
```

```python
import functools
import math

import jax
import jax.numpy as jnp
from jax import lax
from jax.experimental import pallas as pl
from jax.experimental.pallas import tpu as pltpu
from jax.sharding import PartitionSpec as P

SCALING = 2.0

MESH = pl.DeviceIdType.MESH
F32 = jnp.float32
BF16 = jnp.bfloat16


def fused_body(
    replicas,
    tensors,
    owned,
    x_hbm,
    v_hbm,
    w_hbm,
    a_hbm,
    b_hbm,
    ids_hbm,
    table_hbm,
    hid,
    down_ref,
    up_ref,
    x,
    w,
    v_own,
    v_full,
    a_all,
    b_all,
    cu_all,
    cd_all,
    cm,
    cmt,
    part,
    snd,
    hop,
    hold,
    edge,
    up_part,
    up_all,
    cnt_part,
    cnt_all,
    ids_ref,
    table_ref,
    load_sem,
    a_send_r,
    a_send_l,
    a_recv,
    rs_send,
    rs_recv,
    edge_recv,
    b_send,
    b_recv,
    v_send,
    v_recv,
    cu_send,
    cu_recv,
    cd_send,
    cd_recv,
    up_send,
    up_recv,
    cnt_send,
    cnt_recv,
):
    R, T = replicas, tensors
    me = lax.axis_index("replica")
    mt = lax.axis_index("tensor")
    rows = a_hbm.shape[0]
    rank = rows // owned
    tokens, width = x_hbm.shape
    vshare = v_hbm.shape[1]
    adapters = R * owned

    def remote(src, dst, send, recv, axis, to):
        return pltpu.make_async_remote_copy(
            src_ref=src, dst_ref=dst, send_sem=send, recv_sem=recv,
            device_id={axis: to}, device_id_type=MESH,
        )

    def peers(axis):
        n, here = (R, me) if axis == "replica" else (T, mt)
        return [lax.rem(here + d, n) for d in range(1, n)]

    def vcols(i):
        return v_full.at[:, pl.ds(pl.multiple_of(i * vshare, vshare), vshare)]

    loads = {
        "ids": pltpu.make_async_copy(ids_hbm, ids_ref, load_sem.at[7]),
        "table": pltpu.make_async_copy(table_hbm, table_ref, load_sem.at[8]),
        "b": pltpu.make_async_copy(b_hbm, b_all.at[me], load_sem.at[0]),
        "v": pltpu.make_async_copy(v_hbm, v_own, load_sem.at[1]),
        "x": pltpu.make_async_copy(x_hbm, x, load_sem.at[2]),
        "a": pltpu.make_async_copy(a_hbm, a_all.at[me], load_sem.at[3]),
        "vf": pltpu.make_async_copy(v_hbm, vcols(mt), load_sem.at[4]),
        "w": pltpu.make_async_copy(w_hbm, w, load_sem.at[5]),
    }
    for name in ("ids", "table", "b", "v", "x", "a", "vf", "w"):
        loads[name].start()

    barrier = pltpu.get_barrier_semaphore()
    for axis in ("replica", "tensor"):
        for to in peers(axis):
            pl.semaphore_signal(barrier, inc=1, device_id={axis: to}, device_id_type=MESH)

    loads["ids"].wait()
    loads["table"].wait()
    ids = ids_ref[...]
    slot = jnp.zeros_like(ids)
    for i in range(adapters):
        slot = jnp.where(ids == i, table_ref[i], slot)
    slot = jnp.broadcast_to(slot, (rank, tokens))
    pad = cnt_part.shape[1]
    for j in range(R):
        which = lax.broadcasted_iota(jnp.int32, (pad, tokens), 0)
        hit = (slot[0:pad, :] == which + j * owned) & (which < owned)
        total = jnp.sum(hit.astype(F32), axis=1, keepdims=True)
        cnt_part[j] = jnp.broadcast_to(total, (pad, 128))

    pl.semaphore_wait(barrier, R - 1 + T - 1)

    b_out = [
        remote(b_hbm, b_all.at[me], b_send.at[d], b_recv.at[me], "replica", to)
        for d, to in enumerate(peers("replica"))
    ]
    for copy in b_out:
        copy.start()

    def a_right(j, k, src):
        return remote(src, a_all.at[j], a_send_r.at[k], a_recv.at[j], "replica", me + 1)

    def a_left(j, k, src):
        return remote(src, a_all.at[j], a_send_l.at[k], a_recv.at[j], "replica", me - 1)

    @pl.when(me < R - 1)
    def _():
        a_right(me, 0, a_hbm).start()

    @pl.when(me > 0)
    def _():
        a_left(me, 0, a_hbm).start()

    cnt_out = [
        remote(cnt_part.at[to], cnt_all.at[me], cnt_send.at[d], cnt_recv.at[me], "replica", to)
        for d, to in enumerate(peers("replica"))
    ]
    for copy in cnt_out:
        copy.start()
    cnt_all[me] = cnt_part[me]

    loads["b"].wait()
    loads["v"].wait()
    for to in peers("replica"):
        remote(b_hbm, b_all.at[to], b_send.at[0], b_recv.at[to], "replica", to).wait_recv()
    product = lax.dot_general(
        b_all[...].reshape(R * rows, vshare), v_own[...], (((1,), (1,)), ((), ())),
        preferred_element_type=F32,
    )
    cu = jnp.zeros((rank, tokens), F32)
    for s in range(adapters):
        cu = jnp.where(slot == s, product[s * rank:(s + 1) * rank, :], cu)
    cu_all[mt] = cu
    cu_out = [
        remote(cu_all.at[mt], cu_all.at[mt], cu_send.at[d], cu_recv.at[mt], "tensor", to)
        for d, to in enumerate(peers("tensor"))
    ]
    for copy in cu_out:
        copy.start()
    v_out = [
        remote(v_hbm, vcols(mt), v_send.at[d], v_recv.at[mt], "tensor", to)
        for d, to in enumerate(peers("tensor"))
    ]

    def a_hop(k):
        @pl.when(me >= k)
        def _():
            j = me - k
            a_right(j, k, a_all.at[j]).wait_recv()
            if k < R - 1:
                @pl.when(me < R - 1)
                def _():
                    a_right(j, k, a_all.at[j]).start()

        @pl.when(me + k < R)
        def _():
            j = me + k
            a_left(j, k, a_all.at[j]).wait_recv()
            if k < R - 1:
                @pl.when(me > 0)
                def _():
                    a_left(j, k, a_all.at[j]).start()

    def add_cd(j):
        p = lax.dot_general(
            a_all[j], x[...], (((1,), (1,)), ((), ())), preferred_element_type=F32
        )
        acc = cd_all[mt]
        for s in range(owned):
            acc = jnp.where(slot == j * owned + s, p[s * rank:(s + 1) * rank, :], acc)
        cd_all[mt] = acc

    def cd_hop(k):
        @pl.when(me >= k)
        def _():
            add_cd(me - k)

        @pl.when(me + k < R)
        def _():
            add_cd(me + k)

    loads["a"].wait()
    loads["x"].wait()
    a_hop(1)

    for to in peers("tensor"):
        remote(cu_all.at[to], cu_all.at[to], cu_send.at[0], cu_recv.at[to], "tensor", to).wait_recv()
    c = cu_all[0]
    for q in range(1, T):
        c = c + cu_all[q]
    c = c.astype(BF16).astype(F32)
    spread = jnp.concatenate([jnp.where(slot == s, c, 0.0) for s in range(adapters)], axis=0)
    cm[...] = spread.astype(BF16).reshape(R, rows, tokens)

    def rs_to(d):
        return remote(snd.at[d], hop.at[me], rs_send.at[d], rs_recv.at[me], "replica", d)

    def to_next(d, to):
        return remote(snd.at[d], edge.at[d], rs_send.at[d], edge_recv.at[d], "replica", to)

    order = []
    for i in range((R + 1) // 2):
        order += [R - 1 - i] + ([i] if i != R - 1 - i else [])
    for j in order:
        p = jnp.dot(cm[j], x[...], preferred_element_type=F32)

        from_end = ((me == 1) & (j >= 2)) | ((me == R - 2) & (j <= R - 3))
        at_start = (me == 0) & (j >= 2)
        at_stop = (me == R - 1) & (j <= R - 3)

        @pl.when(me == j)
        def _():
            part[...] = p

        @pl.when(from_end)
        def _():
            hold[j] = p

        @pl.when((me != j) & jnp.logical_not(from_end))
        def _():
            snd[j] = p.astype(BF16)

        @pl.when(at_start)
        def _():
            to_next(j, me + 1).start()

        @pl.when(at_stop)
        def _():
            to_next(j, me - 1).start()

        @pl.when((me != j) & jnp.logical_not(from_end | at_start | at_stop))
        def _():
            rs_to(j).start()

    def pass_on(k):
        for mine, j in (((me == 1), R - 1 - k), ((me == R - 2), k)):
            @pl.when(mine)
            def _():
                to_next(j, me).wait_recv()
                snd[j] = (hold[j] + edge[j].astype(F32)).astype(BF16)
                rs_to(j).start()

    for copy in v_out:
        copy.start()
    cd_all[mt] = jnp.zeros((rank, tokens), F32)
    add_cd(me)
    a_hop(2)
    cd_hop(1)
    if R > 2:
        pass_on(0)
    cmt[...] = spread.T.astype(BF16)
    cd_hop(2)
    for k in range(3, R):
        a_hop(k)
        cd_hop(k)
    cd_out = [
        remote(cd_all.at[mt], cd_all.at[mt], cd_send.at[d], cd_recv.at[mt], "tensor", to)
        for d, to in enumerate(peers("tensor"))
    ]
    for copy in cd_out:
        copy.start()

    for k in range(1, R - 2):
        pass_on(k)

    for to in peers("tensor"):
        remote(cd_all.at[to], cd_all.at[to], cd_send.at[0], cd_recv.at[to], "tensor", to).wait_recv()
    c = cd_all[0]
    for q in range(1, T):
        c = c + cd_all[q]
    c = c.astype(BF16).astype(F32)
    spread = jnp.concatenate([jnp.where(slot == s, c, 0.0) for s in range(adapters)], axis=0)
    up_part[...] = jnp.dot(
        spread.astype(BF16), v_own[...], preferred_element_type=F32
    ).reshape(R, rows, vshare)
    up_out = [
        remote(up_part.at[to], up_all.at[me], up_send.at[d], up_recv.at[me], "replica", to)
        for d, to in enumerate(peers("replica"))
    ]
    for copy in up_out:
        copy.start()
    up_all[me] = up_part[me]

    loads["vf"].wait()
    loads["w"].wait()
    for to in peers("tensor"):
        remote(v_hbm, vcols(to), v_send.at[0], v_recv.at[to], "tensor", to).wait_recv()
    tile = 256 if width % 256 == 0 else 128

    @pl.loop(0, width // tile)
    def _(i):
        at = pl.ds(pl.multiple_of(i * tile, tile), tile)
        lora = jnp.dot(
            cmt[...], a_all[:, :, at].reshape(R * rows, tile), preferred_element_type=F32
        ).astype(BF16).astype(F32)
        base = lax.dot_general(
            v_full[...], w[at, :], (((1,), (1,)), ((), ())), preferred_element_type=F32
        )
        hid[:, at] = (base + SCALING * lora).astype(BF16)

    for to in peers("replica"):
        remote(cnt_part.at[to], cnt_all.at[to], cnt_send.at[0], cnt_recv.at[to], "replica", to).wait_recv()
    count = cnt_all[0]
    for j in range(1, R):
        count = count + cnt_all[j]
    count = jnp.where(lax.broadcasted_iota(jnp.int32, count.shape, 0) < owned, count, 1.0)
    factor = SCALING / count

    for j in range(R):
        passed = ((me >= 2) & (j == 0)) | ((me <= R - 3) & (j == R - 1))

        @pl.when((me != j) & jnp.logical_not(passed))
        def _():
            remote(snd.at[j], hop.at[j], rs_send.at[0], rs_recv.at[j], "replica", j).wait_recv()
            part[...] = part[...] + hop[j].astype(F32)

    for s in range(owned):
        at = pl.ds(s * rank, rank)
        down_ref[at, :] = (part[at, :] * factor[s:s + 1, 0:1]).astype(BF16)

    for to in peers("replica"):
        remote(up_part.at[to], up_all.at[to], up_send.at[0], up_recv.at[to], "replica", to).wait_recv()
    total = up_all[0]
    for j in range(1, R):
        total = total + up_all[j]
    for s in range(owned):
        at = slice(s * rank, (s + 1) * rank)
        up_ref[at, :] = (total[at, :] * factor[s:s + 1, 0:1]).astype(BF16)

    for copy in b_out + cnt_out + cu_out + v_out + cd_out + up_out:
        copy.wait_send()
    for k in range(R - 1):
        @pl.when((me >= k) & (me < R - 1))
        def _():
            a_right(me - k, k, a_all.at[me - k]).wait_send()

        @pl.when((me + k < R) & (me > 0))
        def _():
            a_left(me + k, k, a_all.at[me + k]).wait_send()
    for d in range(R):
        @pl.when(me != d)
        def _():
            rs_to(d).wait_send()


def scratch_of(R, T, owned, rank, tokens, width, vshare):
    rows = owned * rank
    features = T * vshare
    pad = -(-owned // 8) * 8
    buffers = [
        ((tokens, width), BF16),
        ((width, features), BF16),
        ((tokens, vshare), BF16),
        ((tokens, features), BF16),
        ((R, rows, width), BF16),
        ((R, rows, vshare), BF16),
        ((T, rank, tokens), F32),
        ((T, rank, tokens), F32),
        ((R, rows, tokens), BF16),
        ((tokens, R * rows), BF16),
        ((rows, width), F32),
        ((R, rows, width), BF16),
        ((R, rows, width), BF16),
        ((R, rows, width), F32),
        ((R, rows, width), BF16),
        ((R, rows, vshare), F32),
        ((R, rows, vshare), F32),
        ((R, pad, 128), F32),
        ((R, pad, 128), F32),
    ]
    sems = [9] + [R] * 6 + [R, R, T, T, T, T, T, T, R, R, R, R]
    size = sum(math.prod(shape) * jnp.dtype(kind).itemsize for shape, kind in buffers)
    small = [pltpu.VMEM((1, tokens), jnp.int32), pltpu.SMEM((R * owned,), jnp.int32)]
    return size, [pltpu.VMEM(*b) for b in buffers] + small + [pltpu.SemaphoreType.DMA((n,)) for n in sems]


VMEM_LIMIT = 60 * 1024 * 1024


def shards(
    hidden_input_saved,
    value_output_gradient,
    frozen_value_weight,
    adapter_lower_factor,
    adapter_upper_factor,
    per_token_adapter,
    adapter_table_slot,
):
    R, T = lax.axis_size("replica"), lax.axis_size("tensor")
    owned, rank, width = adapter_lower_factor.shape
    vshare = adapter_upper_factor.shape[2]
    tokens = hidden_input_saved.shape[0]
    size, scratch = scratch_of(R, T, owned, rank, tokens, width, vshare)
    if size > VMEM_LIMIT // 3:
        return dispatched(
            hidden_input_saved, value_output_gradient, frozen_value_weight,
            adapter_lower_factor, adapter_upper_factor, per_token_adapter, adapter_table_slot,
        )
    rows = owned * rank
    anywhere = pl.BlockSpec(memory_space=pl.ANY)
    vmem = pl.BlockSpec(memory_space=pltpu.VMEM)
    hidden_grad, down_grad, up_grad = pl.pallas_call(
        functools.partial(fused_body, R, T, owned),
        out_shape=(
            pltpu.VMEM((tokens, width), BF16),
            jax.ShapeDtypeStruct((rows, width), BF16),
            jax.ShapeDtypeStruct((rows, vshare), BF16),
        ),
        in_specs=[pl.BlockSpec(memory_space=pltpu.HBM)] * 7,
        out_specs=(vmem, vmem, vmem),
        scratch_shapes=scratch,
        compiler_params=pltpu.CompilerParams(
            collective_id=0, has_side_effects=True, vmem_limit_bytes=VMEM_LIMIT
        ),
        name="lora_value_backward",
    )(
        hidden_input_saved,
        value_output_gradient,
        frozen_value_weight,
        adapter_lower_factor.reshape(rows, width),
        adapter_upper_factor.reshape(rows, vshare),
        per_token_adapter.reshape(1, tokens),
        adapter_table_slot,
    )
    return (
        hidden_grad,
        down_grad.reshape(owned, rank, width),
        up_grad.reshape(owned, rank, vshare),
    )


def dispatched(
    hidden_input_saved,
    value_output_gradient,
    frozen_value_weight,
    adapter_lower_factor,
    adapter_upper_factor,
    per_token_adapter,
    adapter_table_slot,
):
    replicas = lax.axis_size("replica")
    local_owned_count, reduced_rank_product, share_width = adapter_lower_factor.shape
    value_head_share = adapter_upper_factor.shape[2]
    tokens_here = hidden_input_saved.shape[0]
    adapters = local_owned_count * replicas
    capacity = max(2, 3 * tokens_here // adapters)
    slot_total_count = adapters * capacity
    full_grad = lax.all_gather(value_output_gradient, "tensor", axis=1, tiled=True)
    base_grad = lax.dot_general(
        full_grad, frozen_value_weight, (((1,), (1,)), ((), ())), preferred_element_type=jnp.float32
    )
    adapter_ids = per_token_adapter[:, 0]
    catalog = jnp.arange(adapters, dtype=jnp.int32)
    slot_ids = jnp.sum(
        jnp.where(adapter_ids[:, None] == catalog[None, :], adapter_table_slot[None, :], 0), axis=1
    )
    one_hot = (slot_ids[:, None] == catalog[None, :]).astype(jnp.int32)
    position = jnp.sum(one_hot * jnp.cumsum(one_hot, axis=0), axis=1) - 1
    destination_index = slot_ids * capacity + position
    rows_send = (
        jnp.zeros((slot_total_count, share_width), jnp.bfloat16)
        .at[destination_index]
        .set(hidden_input_saved)
    )
    value_send = (
        jnp.zeros((slot_total_count, value_head_share), jnp.bfloat16)
        .at[destination_index]
        .set(value_output_gradient)
    )
    marks_send = (
        jnp.zeros((slot_total_count,), jnp.bfloat16)
        .at[destination_index]
        .set(jnp.ones((tokens_here,), jnp.bfloat16))
    )
    incoming_rows, value_input_rows, marks_in = (
        lax.all_to_all(
            rows_send.reshape(replicas, local_owned_count, capacity, share_width),
            "replica",
            split_axis=0,
            concat_axis=0,
            tiled=True,
        ),
        lax.all_to_all(
            value_send.reshape(replicas, local_owned_count, capacity, value_head_share),
            "replica",
            split_axis=0,
            concat_axis=0,
            tiled=True,
        ),
        lax.all_to_all(
            marks_send.reshape(replicas, local_owned_count, capacity),
            "replica",
            split_axis=0,
            concat_axis=0,
            tiled=True,
        ),
    )
    lower_factor_share = jnp.einsum(
        "woip,osp->oswi", incoming_rows, adapter_lower_factor, preferred_element_type=jnp.float32
    )
    upper_factor_share = jnp.einsum(
        "xluq,liq->lixu", value_input_rows, adapter_upper_factor, preferred_element_type=jnp.float32
    )
    flat_shape = (local_owned_count, reduced_rank_product, replicas * capacity)
    down_sum, up_sum = lax.psum(
        (lower_factor_share.reshape(flat_shape), upper_factor_share.reshape(flat_shape)), "tensor"
    )
    coeff_down = down_sum.reshape(lower_factor_share.shape).astype(jnp.bfloat16)
    upper_coefficient = up_sum.reshape(upper_factor_share.shape).astype(jnp.bfloat16)
    counts = jnp.sum(marks_in.astype(jnp.float32), axis=(0, 2))
    factor = SCALING / counts
    down_grad = (
        jnp.einsum(
            "arnc,nacd->ard", upper_coefficient, incoming_rows, preferred_element_type=jnp.float32
        )
        * factor[:, None, None]
    ).astype(jnp.bfloat16)
    up_grad = (
        jnp.einsum(
            "arnc,nace->are", coeff_down, value_input_rows, preferred_element_type=jnp.float32
        )
        * factor[:, None, None]
    ).astype(jnp.bfloat16)
    coeff_send = jnp.transpose(upper_coefficient, (2, 0, 3, 1))
    coeff_back = lax.all_to_all(
        coeff_send, "replica", split_axis=0, concat_axis=0, tiled=True
    ).reshape(adapters, capacity, reduced_rank_product)
    adapter_token_rows = (
        jnp.einsum(
            "acr,ard->acd",
            coeff_back,
            lax.all_gather(adapter_lower_factor, "replica", axis=0, tiled=True),
            preferred_element_type=jnp.float32,
        )
        .astype(jnp.bfloat16)
        .reshape(slot_total_count, share_width)
    )
    selected_rows = adapter_token_rows[destination_index]
    hidden_grad = (base_grad + SCALING * selected_rows.astype(jnp.float32)).astype(jnp.bfloat16)
    return (hidden_grad, down_grad, up_grad)


def solution(mesh):
    placed = (
        P(("groups", "replica"), "tensor"),
        P(("groups", "replica"), "tensor"),
        P("tensor", None),
        P(("groups", "replica"), None, "tensor"),
        P(("groups", "replica"), None, "tensor"),
        P(("groups", "replica"), None),
        P("groups"),
    )
    return jax.shard_map(
        shards,
        mesh=mesh,
        in_specs=placed,
        out_specs=(
            P(("groups", "replica"), "tensor"),
            P(("groups", "replica"), None, "tensor"),
            P(("groups", "replica"), None, "tensor"),
        ),
        check_vma=False,
    )
```

```python
import functools
import math

import jax
import jax.numpy as jnp
from jax import lax
from jax.experimental import pallas as pl
from jax.experimental.pallas import tpu as pltpu
from jax.sharding import PartitionSpec as P

SCALING = 2.0

MESH = pl.DeviceIdType.MESH
F32 = jnp.float32
BF16 = jnp.bfloat16


def fused_body(
    replicas,
    tensors,
    owned,
    x_hbm,
    v_hbm,
    w_hbm,
    a_hbm,
    b_hbm,
    ids_hbm,
    table_hbm,
    hid,
    down_ref,
    up_ref,
    x,
    w,
    v_own,
    v_full,
    a_all,
    b_all,
    cu_all,
    cd_all,
    cm,
    cmt,
    part,
    snd,
    hop,
    hold,
    edge,
    up_part,
    up_all,
    cnt_part,
    cnt_all,
    ids_ref,
    table_ref,
    load_sem,
    a_send_r,
    a_send_l,
    a_recv,
    rs_send,
    rs_recv,
    edge_recv,
    b_send,
    b_recv,
    v_send,
    v_recv,
    cu_send,
    cu_recv,
    cd_send,
    cd_recv,
    up_send,
    up_recv,
    cnt_send,
    cnt_recv,
):
    R, T = replicas, tensors
    me = lax.axis_index("replica")
    mt = lax.axis_index("tensor")
    rows = a_hbm.shape[0]
    rank = rows // owned
    tokens, width = x_hbm.shape
    vshare = v_hbm.shape[1]
    adapters = R * owned

    def remote(src, dst, send, recv, axis, to):
        return pltpu.make_async_remote_copy(
            src_ref=src, dst_ref=dst, send_sem=send, recv_sem=recv,
            device_id={axis: to}, device_id_type=MESH,
        )

    def peers(axis):
        n, here = (R, me) if axis == "replica" else (T, mt)
        return [lax.rem(here + d, n) for d in range(1, n)]

    def vcols(i):
        return v_full.at[:, pl.ds(pl.multiple_of(i * vshare, vshare), vshare)]

    loads = {
        "ids": pltpu.make_async_copy(ids_hbm, ids_ref, load_sem.at[7]),
        "table": pltpu.make_async_copy(table_hbm, table_ref, load_sem.at[8]),
        "b": pltpu.make_async_copy(b_hbm, b_all.at[me], load_sem.at[0]),
        "v": pltpu.make_async_copy(v_hbm, v_own, load_sem.at[1]),
        "x": pltpu.make_async_copy(x_hbm, x, load_sem.at[2]),
        "a": pltpu.make_async_copy(a_hbm, a_all.at[me], load_sem.at[3]),
        "vf": pltpu.make_async_copy(v_hbm, vcols(mt), load_sem.at[4]),
        "w": pltpu.make_async_copy(w_hbm, w, load_sem.at[5]),
    }
    for name in ("ids", "table", "b", "v", "x", "a", "vf", "w"):
        loads[name].start()

    barrier = pltpu.get_barrier_semaphore()
    for axis in ("replica", "tensor"):
        for to in peers(axis):
            pl.semaphore_signal(barrier, inc=1, device_id={axis: to}, device_id_type=MESH)

    loads["ids"].wait()
    loads["table"].wait()
    ids = ids_ref[...]
    slot = jnp.zeros_like(ids)
    for i in range(adapters):
        slot = jnp.where(ids == i, table_ref[i], slot)
    slot = jnp.broadcast_to(slot, (rank, tokens))
    pad = cnt_part.shape[1]
    for j in range(R):
        which = lax.broadcasted_iota(jnp.int32, (pad, tokens), 0)
        hit = (slot[0:pad, :] == which + j * owned) & (which < owned)
        total = jnp.sum(hit.astype(F32), axis=1, keepdims=True)
        cnt_part[j] = jnp.broadcast_to(total, (pad, 128))

    pl.semaphore_wait(barrier, R - 1 + T - 1)

    b_out = [
        remote(b_hbm, b_all.at[me], b_send.at[d], b_recv.at[me], "replica", to)
        for d, to in enumerate(peers("replica"))
    ]
    for copy in b_out:
        copy.start()

    def a_right(j, k, src):
        return remote(src, a_all.at[j], a_send_r.at[k], a_recv.at[j], "replica", me + 1)

    def a_left(j, k, src):
        return remote(src, a_all.at[j], a_send_l.at[k], a_recv.at[j], "replica", me - 1)

    @pl.when(me < R - 1)
    def _():
        a_right(me, 0, a_hbm).start()

    @pl.when(me > 0)
    def _():
        a_left(me, 0, a_hbm).start()

    cnt_out = [
        remote(cnt_part.at[to], cnt_all.at[me], cnt_send.at[d], cnt_recv.at[me], "replica", to)
        for d, to in enumerate(peers("replica"))
    ]
    for copy in cnt_out:
        copy.start()
    cnt_all[me] = cnt_part[me]

    loads["b"].wait()
    loads["v"].wait()
    for to in peers("replica"):
        remote(b_hbm, b_all.at[to], b_send.at[0], b_recv.at[to], "replica", to).wait_recv()
    product = lax.dot_general(
        b_all[...].reshape(R * rows, vshare), v_own[...], (((1,), (1,)), ((), ())),
        preferred_element_type=F32,
    )
    cu = jnp.zeros((rank, tokens), F32)
    for s in range(adapters):
        cu = jnp.where(slot == s, product[s * rank:(s + 1) * rank, :], cu)
    cu_all[mt] = cu
    cu_out = [
        remote(cu_all.at[mt], cu_all.at[mt], cu_send.at[d], cu_recv.at[mt], "tensor", to)
        for d, to in enumerate(peers("tensor"))
    ]
    for copy in cu_out:
        copy.start()
    v_out = [
        remote(v_hbm, vcols(mt), v_send.at[d], v_recv.at[mt], "tensor", to)
        for d, to in enumerate(peers("tensor"))
    ]

    def a_hop(k):
        @pl.when(me >= k)
        def _():
            j = me - k
            a_right(j, k, a_all.at[j]).wait_recv()
            if k < R - 1:
                @pl.when(me < R - 1)
                def _():
                    a_right(j, k, a_all.at[j]).start()

        @pl.when(me + k < R)
        def _():
            j = me + k
            a_left(j, k, a_all.at[j]).wait_recv()
            if k < R - 1:
                @pl.when(me > 0)
                def _():
                    a_left(j, k, a_all.at[j]).start()

    def add_cd(j):
        p = lax.dot_general(
            a_all[j], x[...], (((1,), (1,)), ((), ())), preferred_element_type=F32
        )
        acc = cd_all[mt]
        for s in range(owned):
            acc = jnp.where(slot == j * owned + s, p[s * rank:(s + 1) * rank, :], acc)
        cd_all[mt] = acc

    def cd_hop(k):
        @pl.when(me >= k)
        def _():
            add_cd(me - k)

        @pl.when(me + k < R)
        def _():
            add_cd(me + k)

    loads["a"].wait()
    loads["x"].wait()
    a_hop(1)

    for to in peers("tensor"):
        remote(cu_all.at[to], cu_all.at[to], cu_send.at[0], cu_recv.at[to], "tensor", to).wait_recv()
    c = cu_all[0]
    for q in range(1, T):
        c = c + cu_all[q]
    c = c.astype(BF16).astype(F32)
    spread = jnp.concatenate([jnp.where(slot == s, c, 0.0) for s in range(adapters)], axis=0)
    cm[...] = spread.astype(BF16).reshape(R, rows, tokens)

    def rs_to(d):
        return remote(snd.at[d], hop.at[me], rs_send.at[d], rs_recv.at[me], "replica", d)

    def to_next(d, to):
        return remote(snd.at[d], edge.at[d], rs_send.at[d], edge_recv.at[d], "replica", to)

    order = []
    for i in range((R + 1) // 2):
        order += [R - 1 - i] + ([i] if i != R - 1 - i else [])
    for j in order:
        p = jnp.dot(cm[j], x[...], preferred_element_type=F32)

        from_end = ((me == 1) & (j >= 2)) | ((me == R - 2) & (j <= R - 3))
        at_start = (me == 0) & (j >= 2)
        at_stop = (me == R - 1) & (j <= R - 3)

        @pl.when(me == j)
        def _():
            part[...] = p

        @pl.when(from_end)
        def _():
            hold[j] = p

        @pl.when((me != j) & jnp.logical_not(from_end))
        def _():
            snd[j] = p.astype(BF16)

        @pl.when(at_start)
        def _():
            to_next(j, me + 1).start()

        @pl.when(at_stop)
        def _():
            to_next(j, me - 1).start()

        @pl.when((me != j) & jnp.logical_not(from_end | at_start | at_stop))
        def _():
            rs_to(j).start()

    def pass_on(k):
        for mine, j in (((me == 1), R - 1 - k), ((me == R - 2), k)):
            @pl.when(mine)
            def _():
                to_next(j, me).wait_recv()
                snd[j] = (hold[j] + edge[j].astype(F32)).astype(BF16)
                rs_to(j).start()

    for copy in v_out:
        copy.start()
    cd_all[mt] = jnp.zeros((rank, tokens), F32)
    add_cd(me)
    a_hop(2)
    cd_hop(1)
    if R > 2:
        pass_on(0)
    cmt[...] = spread.T.astype(BF16)
    cd_hop(2)
    for k in range(3, R):
        a_hop(k)
        cd_hop(k)
    cd_out = [
        remote(cd_all.at[mt], cd_all.at[mt], cd_send.at[d], cd_recv.at[mt], "tensor", to)
        for d, to in enumerate(peers("tensor"))
    ]
    for copy in cd_out:
        copy.start()

    for k in range(1, R - 2):
        pass_on(k)

    for to in peers("tensor"):
        remote(cd_all.at[to], cd_all.at[to], cd_send.at[0], cd_recv.at[to], "tensor", to).wait_recv()
    c = cd_all[0]
    for q in range(1, T):
        c = c + cd_all[q]
    c = c.astype(BF16).astype(F32)
    spread = jnp.concatenate([jnp.where(slot == s, c, 0.0) for s in range(adapters)], axis=0)
    up_part[...] = jnp.dot(
        spread.astype(BF16), v_own[...], preferred_element_type=F32
    ).astype(BF16).reshape(R, rows, vshare)
    up_out = [
        remote(up_part.at[to], up_all.at[me], up_send.at[d], up_recv.at[me], "replica", to)
        for d, to in enumerate(peers("replica"))
    ]
    for copy in up_out:
        copy.start()
    up_all[me] = up_part[me]

    loads["vf"].wait()
    loads["w"].wait()
    for to in peers("tensor"):
        remote(v_hbm, vcols(to), v_send.at[0], v_recv.at[to], "tensor", to).wait_recv()
    tile = 256 if width % 256 == 0 else 128

    @pl.loop(0, width // tile)
    def _(i):
        at = pl.ds(pl.multiple_of(i * tile, tile), tile)
        lora = jnp.dot(
            cmt[...], a_all[:, :, at].reshape(R * rows, tile), preferred_element_type=F32
        ).astype(BF16).astype(F32)
        base = lax.dot_general(
            v_full[...], w[at, :], (((1,), (1,)), ((), ())), preferred_element_type=F32
        )
        hid[:, at] = (base + SCALING * lora).astype(BF16)

    for to in peers("replica"):
        remote(cnt_part.at[to], cnt_all.at[to], cnt_send.at[0], cnt_recv.at[to], "replica", to).wait_recv()
    count = cnt_all[0]
    for j in range(1, R):
        count = count + cnt_all[j]
    count = jnp.where(lax.broadcasted_iota(jnp.int32, count.shape, 0) < owned, count, 1.0)
    factor = SCALING / count

    for j in range(R):
        passed = ((me >= 2) & (j == 0)) | ((me <= R - 3) & (j == R - 1))

        @pl.when((me != j) & jnp.logical_not(passed))
        def _():
            remote(snd.at[j], hop.at[j], rs_send.at[0], rs_recv.at[j], "replica", j).wait_recv()
            part[...] = part[...] + hop[j].astype(F32)

    for s in range(owned):
        at = pl.ds(s * rank, rank)
        down_ref[at, :] = (part[at, :] * factor[s:s + 1, 0:1]).astype(BF16)

    for to in peers("replica"):
        remote(up_part.at[to], up_all.at[to], up_send.at[0], up_recv.at[to], "replica", to).wait_recv()
    total = up_all[0].astype(F32)
    for j in range(1, R):
        total = total + up_all[j].astype(F32)
    for s in range(owned):
        at = slice(s * rank, (s + 1) * rank)
        up_ref[at, :] = (total[at, :] * factor[s:s + 1, 0:1]).astype(BF16)

    for copy in b_out + cnt_out + cu_out + v_out + cd_out + up_out:
        copy.wait_send()
    for k in range(R - 1):
        @pl.when((me >= k) & (me < R - 1))
        def _():
            a_right(me - k, k, a_all.at[me - k]).wait_send()

        @pl.when((me + k < R) & (me > 0))
        def _():
            a_left(me + k, k, a_all.at[me + k]).wait_send()
    for d in range(R):
        @pl.when(me != d)
        def _():
            rs_to(d).wait_send()


def scratch_of(R, T, owned, rank, tokens, width, vshare):
    rows = owned * rank
    features = T * vshare
    pad = -(-owned // 8) * 8
    buffers = [
        ((tokens, width), BF16),
        ((width, features), BF16),
        ((tokens, vshare), BF16),
        ((tokens, features), BF16),
        ((R, rows, width), BF16),
        ((R, rows, vshare), BF16),
        ((T, rank, tokens), F32),
        ((T, rank, tokens), F32),
        ((R, rows, tokens), BF16),
        ((tokens, R * rows), BF16),
        ((rows, width), F32),
        ((R, rows, width), BF16),
        ((R, rows, width), BF16),
        ((R, rows, width), F32),
        ((R, rows, width), BF16),
        ((R, rows, vshare), BF16),
        ((R, rows, vshare), BF16),
        ((R, pad, 128), F32),
        ((R, pad, 128), F32),
    ]
    sems = [9] + [R] * 6 + [R, R, T, T, T, T, T, T, R, R, R, R]
    size = sum(math.prod(shape) * jnp.dtype(kind).itemsize for shape, kind in buffers)
    small = [pltpu.VMEM((1, tokens), jnp.int32), pltpu.SMEM((R * owned,), jnp.int32)]
    return size, [pltpu.VMEM(*b) for b in buffers] + small + [pltpu.SemaphoreType.DMA((n,)) for n in sems]


VMEM_LIMIT = 60 * 1024 * 1024


def shards(
    hidden_input_saved,
    value_output_gradient,
    frozen_value_weight,
    adapter_lower_factor,
    adapter_upper_factor,
    per_token_adapter,
    adapter_table_slot,
):
    R, T = lax.axis_size("replica"), lax.axis_size("tensor")
    owned, rank, width = adapter_lower_factor.shape
    vshare = adapter_upper_factor.shape[2]
    tokens = hidden_input_saved.shape[0]
    size, scratch = scratch_of(R, T, owned, rank, tokens, width, vshare)
    if size > VMEM_LIMIT // 3:
        return dispatched(
            hidden_input_saved, value_output_gradient, frozen_value_weight,
            adapter_lower_factor, adapter_upper_factor, per_token_adapter, adapter_table_slot,
        )
    rows = owned * rank
    anywhere = pl.BlockSpec(memory_space=pl.ANY)
    vmem = pl.BlockSpec(memory_space=pltpu.VMEM)
    hidden_grad, down_grad, up_grad = pl.pallas_call(
        functools.partial(fused_body, R, T, owned),
        out_shape=(
            pltpu.VMEM((tokens, width), BF16),
            jax.ShapeDtypeStruct((rows, width), BF16),
            jax.ShapeDtypeStruct((rows, vshare), BF16),
        ),
        in_specs=[pl.BlockSpec(memory_space=pltpu.HBM)] * 7,
        out_specs=(vmem, vmem, vmem),
        scratch_shapes=scratch,
        compiler_params=pltpu.CompilerParams(
            collective_id=0, has_side_effects=True, vmem_limit_bytes=VMEM_LIMIT
        ),
        name="lora_value_backward",
    )(
        hidden_input_saved,
        value_output_gradient,
        frozen_value_weight,
        adapter_lower_factor.reshape(rows, width),
        adapter_upper_factor.reshape(rows, vshare),
        per_token_adapter.reshape(1, tokens),
        adapter_table_slot,
    )
    return (
        hidden_grad,
        down_grad.reshape(owned, rank, width),
        up_grad.reshape(owned, rank, vshare),
    )


def dispatched(
    hidden_input_saved,
    value_output_gradient,
    frozen_value_weight,
    adapter_lower_factor,
    adapter_upper_factor,
    per_token_adapter,
    adapter_table_slot,
):
    replicas = lax.axis_size("replica")
    local_owned_count, reduced_rank_product, share_width = adapter_lower_factor.shape
    value_head_share = adapter_upper_factor.shape[2]
    tokens_here = hidden_input_saved.shape[0]
    adapters = local_owned_count * replicas
    capacity = max(2, 3 * tokens_here // adapters)
    slot_total_count = adapters * capacity
    full_grad = lax.all_gather(value_output_gradient, "tensor", axis=1, tiled=True)
    base_grad = lax.dot_general(
        full_grad, frozen_value_weight, (((1,), (1,)), ((), ())), preferred_element_type=jnp.float32
    )
    adapter_ids = per_token_adapter[:, 0]
    catalog = jnp.arange(adapters, dtype=jnp.int32)
    slot_ids = jnp.sum(
        jnp.where(adapter_ids[:, None] == catalog[None, :], adapter_table_slot[None, :], 0), axis=1
    )
    one_hot = (slot_ids[:, None] == catalog[None, :]).astype(jnp.int32)
    position = jnp.sum(one_hot * jnp.cumsum(one_hot, axis=0), axis=1) - 1
    destination_index = slot_ids * capacity + position
    rows_send = (
        jnp.zeros((slot_total_count, share_width), jnp.bfloat16)
        .at[destination_index]
        .set(hidden_input_saved)
    )
    value_send = (
        jnp.zeros((slot_total_count, value_head_share), jnp.bfloat16)
        .at[destination_index]
        .set(value_output_gradient)
    )
    marks_send = (
        jnp.zeros((slot_total_count,), jnp.bfloat16)
        .at[destination_index]
        .set(jnp.ones((tokens_here,), jnp.bfloat16))
    )
    incoming_rows, value_input_rows, marks_in = (
        lax.all_to_all(
            rows_send.reshape(replicas, local_owned_count, capacity, share_width),
            "replica",
            split_axis=0,
            concat_axis=0,
            tiled=True,
        ),
        lax.all_to_all(
            value_send.reshape(replicas, local_owned_count, capacity, value_head_share),
            "replica",
            split_axis=0,
            concat_axis=0,
            tiled=True,
        ),
        lax.all_to_all(
            marks_send.reshape(replicas, local_owned_count, capacity),
            "replica",
            split_axis=0,
            concat_axis=0,
            tiled=True,
        ),
    )
    lower_factor_share = jnp.einsum(
        "woip,osp->oswi", incoming_rows, adapter_lower_factor, preferred_element_type=jnp.float32
    )
    upper_factor_share = jnp.einsum(
        "xluq,liq->lixu", value_input_rows, adapter_upper_factor, preferred_element_type=jnp.float32
    )
    flat_shape = (local_owned_count, reduced_rank_product, replicas * capacity)
    down_sum, up_sum = lax.psum(
        (lower_factor_share.reshape(flat_shape), upper_factor_share.reshape(flat_shape)), "tensor"
    )
    coeff_down = down_sum.reshape(lower_factor_share.shape).astype(jnp.bfloat16)
    upper_coefficient = up_sum.reshape(upper_factor_share.shape).astype(jnp.bfloat16)
    counts = jnp.sum(marks_in.astype(jnp.float32), axis=(0, 2))
    factor = SCALING / counts
    down_grad = (
        jnp.einsum(
            "arnc,nacd->ard", upper_coefficient, incoming_rows, preferred_element_type=jnp.float32
        )
        * factor[:, None, None]
    ).astype(jnp.bfloat16)
    up_grad = (
        jnp.einsum(
            "arnc,nace->are", coeff_down, value_input_rows, preferred_element_type=jnp.float32
        )
        * factor[:, None, None]
    ).astype(jnp.bfloat16)
    coeff_send = jnp.transpose(upper_coefficient, (2, 0, 3, 1))
    coeff_back = lax.all_to_all(
        coeff_send, "replica", split_axis=0, concat_axis=0, tiled=True
    ).reshape(adapters, capacity, reduced_rank_product)
    adapter_token_rows = (
        jnp.einsum(
            "acr,ard->acd",
            coeff_back,
            lax.all_gather(adapter_lower_factor, "replica", axis=0, tiled=True),
            preferred_element_type=jnp.float32,
        )
        .astype(jnp.bfloat16)
        .reshape(slot_total_count, share_width)
    )
    selected_rows = adapter_token_rows[destination_index]
    hidden_grad = (base_grad + SCALING * selected_rows.astype(jnp.float32)).astype(jnp.bfloat16)
    return (hidden_grad, down_grad, up_grad)


def solution(mesh):
    placed = (
        P(("groups", "replica"), "tensor"),
        P(("groups", "replica"), "tensor"),
        P("tensor", None),
        P(("groups", "replica"), None, "tensor"),
        P(("groups", "replica"), None, "tensor"),
        P(("groups", "replica"), None),
        P("groups"),
    )
    return jax.shard_map(
        shards,
        mesh=mesh,
        in_specs=placed,
        out_specs=(
            P(("groups", "replica"), "tensor"),
            P(("groups", "replica"), None, "tensor"),
            P(("groups", "replica"), None, "tensor"),
        ),
        check_vma=False,
    )
```
